32 devices in a mesh: head: 4 (over z), page: 8 (over y, x, core).
Axes of the slice: x: 2, y: 2, z: 4, core: 2. Of those that a mesh axis runs over, the one named last changes fastest.
Arguments:
- hidden: bfloat16 [1024, 4096], P('page', 'head'), may hold values from -6 to 6
- group_qkv: bfloat16 [1024, 6144], P('page', 'head'), may hold values from -2400 to 2400
- mlp_branch: bfloat16 [1024, 4096], P('page', 'head'), may hold values from -6 to 6
- key_cache: bfloat16 [104, 128, 2048], P('page', None, 'head'), may hold values from -6 to 6
- paged_value_cache: bfloat16 [104, 128, 2048], P('page', None, 'head'), may hold values from -6 to 6
- cache_lengths: int32 [2], replicated, may hold values from 2 to 4096, as said below
- page_table: int32 [2, 36], replicated, may hold values from 0 to 103, as said below
- dense_weight: bfloat16 [2048, 4096], P('head'), may hold values from -0.125 to 0.125
- dense_bias: float32 [4096], replicated, may hold values from -3 to 3
- norm_gain: float32 [4096], replicated, may hold values from 0.1 to 1.9
- norm_bias: float32 [4096], replicated, may hold values from -3 to 3
- qkv_weight: bfloat16 [4096, 6144], P(None, 'head'), may hold values from -0.09375 to 0.09375
- qkv_bias: float32 [6144], P('head'), may hold values from -3 to 3
Outputs:
- new_hidden: bfloat16 [1024, 4096], P('page', 'head')
- next_qkv: bfloat16 [1024, 6144], P('page', 'head')
- key_out: bfloat16 [104, 128, 2048], P('page', None, 'head')
- value_out: bfloat16 [104, 128, 2048], P('page', None, 'head')
The draws below stay inside these ranges and needn't reach their ends.
Inputs may be any that keep to these rules, and one draw needn't show every extreme that they name: `cache_lengths`: one request has exactly 4096 cached positions and another exactly 2. `page_table`: all entries are distinct slots; slot s lies on index s // 13 of page.
All inputs are finite; a program needn't handle non-finite values.
Results may differ from the reference program's by a relative error of at most 0.0075.
Values may be sent and summed in bfloat16 or wider, within the bound.
A program may use at most 192 MiB of HBM per device.

```python
import math
import jax
import jax.numpy as jnp
from jax import lax

D = 4096
HALF_HEADS = 16
HEAD_SIZE = 128
ROT = 32
PAGE_TOKENS = 128
GROUP = 512
MAXLEN = 4096
TOKENS = 1024
REQS = 2
MAXP = 36
TOTAL_SLOTS = 104


def table_of(key):
    permuted_slots = jax.random.permutation(jax.random.fold_in(key, 11), TOTAL_SLOTS)
    return permuted_slots[:REQS * MAXP].reshape(REQS, MAXP).astype(jnp.int32)


def keys_of(key):
    gaussian_sample = jax.random.truncated_normal(jax.random.fold_in(key, 14), -6.0, 6.0, (TOTAL_SLOTS, PAGE_TOKENS, HALF_HEADS * HEAD_SIZE), jnp.float32)
    return gaussian_sample


def draw_page_table(key, part):
    return table_of(key)


def draw_cache_lengths(key, part):
    base_lengths = jax.random.randint(jax.random.fold_in(key, 12), (REQS,), 2, MAXLEN + 1)
    shuffled = jax.random.permutation(jax.random.fold_in(key, 13), REQS)
    return base_lengths.at[shuffled[0]].set(MAXLEN).at[shuffled[1]].set(2).astype(jnp.int32)


def draw_key_cache(key, part):
    return keys_of(key).astype(jnp.bfloat16)


def draw_group_qkv(key, part):
    gaussian_sample = jax.random.truncated_normal(jax.random.fold_in(key, 15), -6.0, 6.0, (REQS, GROUP, HALF_HEADS, 3, HEAD_SIZE), jnp.float32)
    return gaussian_sample.reshape(TOKENS, HALF_HEADS * 3 * HEAD_SIZE).astype(jnp.bfloat16)


def steps_of(stream_key, extent, shards, least, largest):
    def one(dim, shards_of):
        steps = jax.random.uniform(jax.random.fold_in(jax.random.fold_in(stream_key, 6), dim), (shards_of,), jnp.float32, least / len(shards), largest / len(shards))
        return jnp.repeat(jnp.exp(steps), extent[dim] // shards_of).reshape((-1,) + (1,) * (len(extent) - dim - 1))

    factor_of = one(*shards[0])
    for cut in shards[1:]:
        factor_of = factor_of * one(*cut)
    return factor_of


def normal_values(rng, extent, spread, limit, cuts=(), held_as=jnp.bfloat16):
    gain = steps_of(rng, extent, cuts, -0.22, 0.18) if cuts else 1.0
    values = jax.random.normal(rng, extent, jnp.float32) * spread * gain
    return jnp.minimum(jnp.maximum(values, -limit), limit).astype(held_as)


def setup_inputs(seed: int = 0) -> dict:
    splits = jax.random.split(jax.random.key(seed), 14)
    return {
        "hidden": normal_values(splits[0], (TOKENS, D), 1.0, 6.0, ((0, 8), (1, 4))),
        "group_qkv": draw_group_qkv(jax.random.fold_in(splits[13], 71), 0),
        "mlp_branch": normal_values(splits[2], (TOKENS, D), 1.0, 6.0, ((0, 8), (1, 4))),
        "key_cache": draw_key_cache(jax.random.fold_in(splits[13], 71), 0),
        "paged_value_cache": normal_values(splits[4], (TOTAL_SLOTS, PAGE_TOKENS, HALF_HEADS * HEAD_SIZE), 1.0, 6.0, ((0, 8), (2, 4))),
        "cache_lengths": draw_cache_lengths(jax.random.fold_in(splits[13], 71), 0),
        "page_table": draw_page_table(jax.random.fold_in(splits[13], 71), 0),
        "dense_weight": normal_values(splits[7], (HALF_HEADS * HEAD_SIZE, D), (HALF_HEADS * HEAD_SIZE) ** -0.5, 0.125, ((0, 4),)),
        "dense_bias": normal_values(splits[8], (D,), 0.5, 3.0, (), jnp.float32),
        "norm_gain": jnp.clip(1.0 + 0.18 * jax.random.normal(splits[9], (D,), jnp.float32), 0.1, 1.9),
        "norm_bias": normal_values(splits[10], (D,), 0.5, 3.0, (), jnp.float32),
        "qkv_weight": normal_values(splits[11], (D, HALF_HEADS * 3 * HEAD_SIZE), D ** -0.5, 0.09375, ((1, 4),)),
        "qkv_bias": normal_values(splits[12], (HALF_HEADS * 3 * HEAD_SIZE,), 0.5, 3.0, ((0, 4),), jnp.float32),
    }


def rotate_rows(inputs, positions):
    half_rot = ROT // 2
    inverse = 1.0 / 10000.0 ** (jnp.arange(0, ROT, 2, dtype=jnp.float32) / ROT)
    angles = positions.astype(jnp.float32)[:, None] * inverse[None, :]
    cosine = jnp.cos(angles)[:, None, :]
    sine_part = jnp.sin(angles)[:, None, :]
    first_half = inputs[..., :half_rot]
    second_half = inputs[..., half_rot:ROT]
    return jnp.concatenate([first_half * cosine - second_half * sine_part, second_half * cosine + first_half * sine_part, inputs[..., ROT:]], axis=-1)

def reference(hidden, group_qkv, mlp_branch, key_cache, paged_value_cache, cache_lengths, page_table, dense_weight, dense_bias, norm_gain, norm_bias, qkv_weight, qkv_bias):
    triples = group_qkv.astype(jnp.float32).reshape(TOKENS, HALF_HEADS, 3, HEAD_SIZE)
    row_ids = jnp.arange(TOKENS, dtype=jnp.int32)
    owner_id = row_ids // GROUP
    positions = cache_lengths[owner_id] + row_ids % GROUP
    queries = rotate_rows(triples[:, :, 0], positions).astype(jnp.bfloat16)
    new_keys = rotate_rows(triples[:, :, 1], positions).astype(jnp.bfloat16)
    new_values = group_qkv.reshape(TOKENS, HALF_HEADS, 3, HEAD_SIZE)[:, :, 2]
    slot_ids = page_table[owner_id, positions // PAGE_TOKENS]
    row_in_page = positions % PAGE_TOKENS
    key_out = key_cache.at[slot_ids, row_in_page].set(new_keys.reshape(TOKENS, HALF_HEADS * HEAD_SIZE))
    value_out = paged_value_cache.at[slot_ids, row_in_page].set(new_values.reshape(TOKENS, HALF_HEADS * HEAD_SIZE))
    score_scale = 1.0 / math.sqrt(HEAD_SIZE)

    def one_request(request_id):
        pages_of = page_table[request_id]
        kept_keys = key_out[pages_of].reshape(MAXP * PAGE_TOKENS, HALF_HEADS, HEAD_SIZE).astype(jnp.float32)
        kept_values = value_out[pages_of].reshape(MAXP * PAGE_TOKENS, HALF_HEADS, HEAD_SIZE).astype(jnp.float32)
        query_block = lax.dynamic_slice_in_dim(queries, request_id * GROUP, GROUP, 0).astype(jnp.float32)
        scores = jnp.einsum('chd,thd->hct', query_block, kept_keys) * score_scale
        length = cache_lengths[request_id]
        visible = jnp.arange(MAXP * PAGE_TOKENS, dtype=jnp.int32)[None, :] <= length + jnp.arange(GROUP, dtype=jnp.int32)[:, None]
        row_peak = lax.optimization_barrier(jnp.max(jnp.where(visible[None], scores, -1e+30), axis=2, keepdims=True))
        weights = jnp.where(visible[None], jnp.exp(scores - row_peak), 0.0)
        rounded = lax.optimization_barrier(weights.astype(jnp.bfloat16)).astype(jnp.float32)
        totals = lax.optimization_barrier(jnp.sum(weights, axis=2)).T
        weighted = jnp.einsum('hct,thd->chd', rounded, kept_values)
        return (weighted / totals[:, :, None]).reshape(GROUP, HALF_HEADS * HEAD_SIZE).astype(jnp.bfloat16)
    attention = lax.map(one_request, jnp.arange(REQS, dtype=jnp.int32)).reshape(TOKENS, HALF_HEADS * HEAD_SIZE)
    projected = jnp.dot(attention, dense_weight, preferred_element_type=jnp.float32)
    stream = (projected + dense_bias + hidden.astype(jnp.float32) + mlp_branch.astype(jnp.float32)).astype(jnp.bfloat16)
    widened = stream.astype(jnp.float32)
    row_mean = lax.optimization_barrier(jnp.sum(widened, axis=1)) / D
    variance = lax.optimization_barrier(jnp.sum(widened * widened, axis=1)) / D - row_mean * row_mean
    normed = ((widened - row_mean[:, None]) * lax.rsqrt(variance[:, None] + 1e-05) * norm_gain + norm_bias).astype(jnp.bfloat16)
    next_qkv = (jnp.dot(normed, qkv_weight, preferred_element_type=jnp.float32) + qkv_bias).astype(jnp.bfloat16)
    return (stream, next_qkv, key_out, value_out)
```

```python
import functools
import math

import jax
import jax.numpy as jnp
from jax import lax
from jax.experimental import pallas as pl
from jax.experimental.pallas import tpu as pltpu
from jax.sharding import PartitionSpec as P

HEAD_SIZE = 128
ROT = 32
PAGE_TOKENS = 128
GROUP = 512
MESH = pl.DeviceIdType.MESH
FLOOR = -1e29
MASKED = -1e30
LIMIT = 56 * 1024 * 1024
BF16 = jnp.bfloat16
F32 = jnp.float32


def greet(axes):
    barrier = pltpu.get_barrier_semaphore()
    count = 0
    for axis in axes:
        size = lax.axis_size(axis)
        me = lax.axis_index(axis)
        for offset in range(1, size):
            pl.semaphore_signal(
                barrier,
                inc=1,
                device_id={axis: lax.rem(me + offset, size)},
                device_id_type=MESH,
            )
            count += 1
    pl.semaphore_wait(barrier, count)


def gather_kernel(heads, x_ref, table_ref, q_ref, kv_ref, q_mine, kv_mine, send, recv, fsend, frecv, lsem):
    pages = lax.axis_size("page")
    chips = pages // 2
    me = lax.axis_index("page")
    chip = lax.div(me, 2)
    core = lax.rem(me, 2)
    sibling = chip * 2 + 1 - core
    rows = x_ref.shape[0]
    width = heads * HEAD_SIZE
    lane = lax.broadcasted_iota(jnp.int32, (rows, HEAD_SIZE), 1)

    def rotated(column):
        x = x_ref[:, column : column + HEAD_SIZE].astype(F32)
        ahead = pltpu.roll(x, HEAD_SIZE - ROT // 2, 1)
        behind = pltpu.roll(x, ROT // 2, 1)
        other = jnp.where(lane < ROT // 2, ahead, behind)
        return (x * table_ref[0] + other * table_ref[1]).astype(BF16)

    for head in range(heads):
        base = head * 3 * HEAD_SIZE
        at = head * HEAD_SIZE
        q_mine[:, at : at + HEAD_SIZE] = rotated(base)
        kv_mine[:, at : at + HEAD_SIZE] = rotated(base + HEAD_SIZE)
        kv_mine[:, width + at : width + at + HEAD_SIZE] = x_ref[
            :, base + 2 * HEAD_SIZE : base + 3 * HEAD_SIZE
        ]

    def block_of(ref, index):
        return ref.at[pl.ds(pl.multiple_of(index * rows, rows), rows), :]

    mine = ((q_mine, q_ref), (kv_mine, kv_ref))
    local = []
    for which, (src, dst) in enumerate(mine):
        copy = pltpu.make_async_copy(src, block_of(dst, me), lsem.at[which])
        copy.start()
        local.append(copy)
    greet(("page",))
    first, forwards = [], []
    for which, (src, dst) in enumerate(mine):
        for offset in range(1, chips):
            target = lax.rem(chip + offset, chips) * 2 + core
            copy = pltpu.make_async_remote_copy(
                src_ref=src,
                dst_ref=block_of(dst, me),
                send_sem=send.at[which, offset],
                recv_sem=recv.at[which, offset],
                device_id={"page": target},
                device_id_type=MESH,
            )
            copy.start()
            first.append(copy)
        copy = pltpu.make_async_remote_copy(
            src_ref=src,
            dst_ref=block_of(dst, me),
            send_sem=fsend.at[which, 0],
            recv_sem=frecv.at[which, 0],
            device_id={"page": sibling},
            device_id_type=MESH,
        )
        copy.start()
        forwards.append(copy)
    for which, (src, dst) in enumerate(mine):
        for offset in range(1, chips):
            source = lax.rem(chip + chips - offset, chips) * 2 + core
            landed = block_of(dst, source)
            pltpu.make_async_remote_copy(
                src_ref=src,
                dst_ref=landed,
                send_sem=send.at[which, offset],
                recv_sem=recv.at[which, offset],
                device_id={"page": source},
                device_id_type=MESH,
            ).wait_recv()
            copy = pltpu.make_async_remote_copy(
                src_ref=landed,
                dst_ref=landed,
                send_sem=fsend.at[which, offset],
                recv_sem=frecv.at[which, offset],
                device_id={"page": sibling},
                device_id_type=MESH,
            )
            copy.start()
            forwards.append(copy)
    for copy in local:
        copy.wait()
    for copy in first:
        copy.wait_send()
    for copy in forwards:
        copy.wait()


def attention_kernel(
    heads, factor,
    req_ref, page_ref, len_ref, flag_ref,
    q_ref, kv_ref, kc_ref, vc_ref,
    ko_ref, vo_ref, o_ref, st_ref,
    acc, m_s, l_s,
):
    slot = pl.program_id(0)
    requests = acc.shape[0]
    width = heads * HEAD_SIZE
    tok_dev = o_ref.shape[2]

    @pl.when(slot == 0)
    def _():
        acc[...] = jnp.zeros_like(acc)
        m_s[...] = jnp.full_like(m_s, FLOOR)
        l_s[...] = jnp.zeros_like(l_s)

    request = req_ref[slot]
    start = page_ref[slot] * PAGE_TOKENS - len_ref[slot]
    flag = flag_ref[slot]
    mine = pl.ds(pl.multiple_of(request * GROUP, GROUP), GROUP)

    @pl.when(flag < 2)
    def _():
        ko_ref[...] = kc_ref[...]
        vo_ref[...] = vc_ref[...]

    @pl.when(flag == 2)
    def _():
        row = start + lax.broadcasted_iota(jnp.int32, (PAGE_TOKENS, GROUP), 0)
        column = lax.broadcasted_iota(jnp.int32, (PAGE_TOKENS, GROUP), 1)
        pick = jnp.where(row == column, 1.0, 0.0).astype(BF16)
        place = start + lax.broadcasted_iota(jnp.int32, (PAGE_TOKENS, width), 0)
        fresh = (place >= 0) & (place < GROUP)
        for part, (old, new) in enumerate(((kc_ref, ko_ref), (vc_ref, vo_ref))):
            moved = jnp.dot(
                pick, kv_ref[mine, part * width : (part + 1) * width], preferred_element_type=F32
            )
            new[0] = jnp.where(fresh, moved, old[0].astype(F32)).astype(BF16)

    def attend(masked):
        for head in range(heads):
            at = slice(head * HEAD_SIZE, (head + 1) * HEAD_SIZE)
            scores = (
                lax.dot_general(
                    ko_ref[0, :, at], q_ref[mine, at], (((1,), (1,)), ((), ())),
                    preferred_element_type=F32,
                )
                * factor
            )
            if masked:
                row = start + lax.broadcasted_iota(jnp.int32, scores.shape, 0)
                column = lax.broadcasted_iota(jnp.int32, scores.shape, 1)
                scores = jnp.where(row <= column, scores, MASKED)
            m_old = m_s[request, head : head + 1, :]
            m_new = jnp.maximum(m_old, jnp.max(scores, axis=0, keepdims=True))
            fade = jnp.exp2(m_old - m_new)
            weights = jnp.exp2(scores - m_new)
            m_s[request, head : head + 1, :] = m_new
            l_s[request, head : head + 1, :] = l_s[request, head : head + 1, :] * fade + jnp.sum(
                weights, axis=0, keepdims=True
            )
            part = lax.dot_general(
                vo_ref[0, :, at], weights.astype(BF16), (((0,), (0,)), ((), ())),
                preferred_element_type=F32,
            )
            acc[request, at, :] = acc[request, at, :] * fade + part

    pl.when((flag >= 1) & (start <= -PAGE_TOKENS))(lambda: attend(False))
    pl.when((flag >= 1) & (start > -PAGE_TOKENS))(lambda: attend(True))

    @pl.when(slot == pl.num_programs(0) - 1)
    def _():
        per = GROUP // tok_dev
        for r in range(requests):
            for b in range(per):
                columns = slice(b * tok_dev, (b + 1) * tok_dev)
                o_ref[r * per + b] = acc[r, :, columns].astype(BF16)
                st_ref[r * per + b, 0:8, :] = m_s[r, :, columns]
                st_ref[r * per + b, 8:16, :] = l_s[r, :, columns]


def tail_kernel(
    heads,
    o_ref, st_ref, hidden_ref, branch_ref, dw_ref, dbias_ref, gain_ref, nbias_ref, qw_ref, qbias_ref,
    hid_out, qkv_out,
    o_in, st_in, dw, qw, att, proj, proj_in, stream, normed, total,
    wsem, osend, orecv, ssend, srecv, psend, precv, gsend, grecv,
):
    pages = lax.axis_size("page")
    shares = lax.axis_size("head")
    me = lax.axis_index("page")
    mz = lax.axis_index("head")
    share = hidden_ref.shape[1]
    model = share * shares

    load_dw = pltpu.make_async_copy(dw_ref, dw, wsem.at[0])
    load_qw = pltpu.make_async_copy(qw_ref, qw, wsem.at[1])
    load_dw.start()
    greet(("page", "head"))

    copies = []
    for offset in range(1, pages):
        target = lax.rem(me + offset, pages)
        for src, dst, ss, rs in ((st_ref, st_in, ssend, srecv), (o_ref, o_in, osend, orecv)):
            copy = pltpu.make_async_remote_copy(
                src_ref=src.at[target],
                dst_ref=dst.at[offset],
                send_sem=ss.at[offset],
                recv_sem=rs.at[offset],
                device_id={"page": target},
                device_id_type=MESH,
            )
            copy.start()
            copies.append(copy)
    load_qw.start()
    st_in[0] = st_ref[me]
    o_in[0] = o_ref[me]
    for copy in copies:
        copy.wait()

    def combine(head):
        rows = pl.ds(pl.multiple_of(head * HEAD_SIZE, HEAD_SIZE), HEAD_SIZE)

        def raise_peak(j, peak):
            return jnp.maximum(peak, st_in[j, pl.ds(head, 1), :])

        peak = lax.fori_loop(0, pages, raise_peak, jnp.full((1, o_in.shape[2]), FLOOR, F32))

        def add(j, pair):
            summed, count = pair
            scale = jnp.exp2(st_in[j, pl.ds(head, 1), :] - peak)
            return (
                summed + o_in[j, rows, :].astype(F32) * scale,
                count + st_in[j, pl.ds(8 + head, 1), :] * scale,
            )

        summed, count = lax.fori_loop(
            0,
            pages,
            add,
            (jnp.zeros((HEAD_SIZE, o_in.shape[2]), F32), jnp.zeros((1, o_in.shape[2]), F32)),
        )
        att[rows, :] = (summed / count).astype(BF16)

    for head in range(heads):
        combine(head)
    load_dw.wait()

    def project(share_index):
        columns = pl.ds(pl.multiple_of(share_index * share, share), share)
        return lax.dot_general(
            att[...], dw[:, columns], (((0,), (0,)), ((), ())), preferred_element_type=F32
        )

    sums = []
    for offset in range(1, shares):
        target = lax.rem(mz + offset, shares)
        proj[offset] = project(target).astype(BF16)
        copy = pltpu.make_async_remote_copy(
            src_ref=proj.at[offset],
            dst_ref=proj_in.at[offset],
            send_sem=psend.at[offset],
            recv_sem=precv.at[offset],
            device_id={"head": target},
            device_id_type=MESH,
        )
        copy.start()
        sums.append(copy)
    my_columns = pl.ds(pl.multiple_of(mz * share, share), share)
    total[...] = (
        project(mz)
        + dbias_ref[:, my_columns]
        + hidden_ref[...].astype(F32)
        + branch_ref[...].astype(F32)
    )
    for offset in range(1, shares):
        sums[offset - 1].wait()
        total[...] += proj_in[offset].astype(F32)
    mine = total[...].astype(BF16)
    hid_out[...] = mine
    stream[mz] = mine
    gathers = []
    for offset in range(1, shares):
        copy = pltpu.make_async_remote_copy(
            src_ref=hid_out,
            dst_ref=stream.at[mz],
            send_sem=gsend.at[offset],
            recv_sem=grecv.at[offset],
            device_id={"head": lax.rem(mz + offset, shares)},
            device_id_type=MESH,
        )
        copy.start()
        gathers.append(copy)
    load_qw.wait()
    for copy in gathers:
        copy.wait()

    rows = hidden_ref.shape[0]

    def moments(j, pair):
        x = stream[j].astype(F32)
        return (
            pair[0] + jnp.sum(x, axis=1, keepdims=True),
            pair[1] + jnp.sum(x * x, axis=1, keepdims=True),
        )

    first, second = lax.fori_loop(
        0, shares, moments, (jnp.zeros((rows, 1), F32), jnp.zeros((rows, 1), F32))
    )
    mean = first / model
    scale = lax.rsqrt(second / model - mean * mean + 1e-05)
    for j in range(shares):
        columns = slice(j * share, (j + 1) * share)
        x = stream[j].astype(F32)
        normed[:, columns] = ((x - mean) * scale * gain_ref[:, columns] + nbias_ref[:, columns]).astype(BF16)

    block = 256
    for j in range(qkv_out.shape[1] // block):
        columns = slice(j * block, (j + 1) * block)
        out = jnp.dot(normed[...], qw[:, columns], preferred_element_type=F32)
        qkv_out[:, columns] = (out + qbias_ref[:, columns]).astype(BF16)


def lookup(table_values, index_rows, count_all):
    matched = index_rows[..., None] == jnp.arange(count_all, dtype=jnp.int32)
    return jnp.sum(jnp.where(matched, table_values, 0), axis=-1)


def on_device(
    hidden, group_qkv, mlp_branch, key_cache, paged_value_cache, cache_lengths, page_table,
    dense_weight, dense_bias, norm_gain, norm_bias, qkv_weight, qkv_bias,
):
    tok_dev, share = hidden.shape
    pages = lax.axis_size("page")
    shares = lax.axis_size("head")
    me = lax.axis_index("page")
    requests = cache_lengths.shape[0]
    max_pages = page_table.shape[1]
    slots = key_cache.shape[0]
    heads = group_qkv.shape[1] // (3 * HEAD_SIZE)
    width = heads * HEAD_SIZE
    every = tok_dev * pages
    vmem = pl.BlockSpec(memory_space=pltpu.VMEM)
    anywhere = pl.BlockSpec(memory_space=pl.ANY)
    dma = pltpu.SemaphoreType.DMA

    global_rows = me * tok_dev + jnp.arange(tok_dev, dtype=jnp.int32)
    positions = lookup(cache_lengths, global_rows // GROUP, requests) + global_rows % GROUP
    lane = jnp.arange(HEAD_SIZE, dtype=jnp.int32)
    half = ROT // 2
    inverse = 1.0 / 10000.0 ** ((2 * (lane % half)).astype(F32) / ROT)
    angles = positions.astype(F32)[:, None] * inverse[None, :]
    turned = lane[None, :] < ROT
    sine = jnp.sin(angles)
    table = jnp.stack(
        [
            jnp.where(turned, jnp.cos(angles), 1.0),
            jnp.where(turned, jnp.where(lane[None, :] < half, -sine, sine), 0.0),
        ]
    )

    q_all, kv_all = pl.pallas_call(
        functools.partial(gather_kernel, heads),
        out_shape=(
            jax.ShapeDtypeStruct((every, width), BF16),
            jax.ShapeDtypeStruct((every, 2 * width), BF16),
        ),
        in_specs=[vmem, vmem],
        out_specs=(anywhere, anywhere),
        scratch_shapes=[
            pltpu.VMEM((tok_dev, width), BF16),
            pltpu.VMEM((tok_dev, 2 * width), BF16),
            dma((2, pages // 2)),
            dma((2, pages // 2)),
            dma((2, pages // 2)),
            dma((2, pages // 2)),
            dma((2,)),
        ],
        compiler_params=pltpu.CompilerParams(
            collective_id=0, has_side_effects=True, vmem_limit_bytes=LIMIT
        ),
        name="gather_qkv",
    )(group_qkv, table)

    slot_ids = me * slots + jnp.arange(slots, dtype=jnp.int32)
    matches = page_table[None, :, :] == slot_ids[:, None, None]
    is_held = jnp.any(matches, axis=(1, 2))
    codes = (
        jnp.arange(requests, dtype=jnp.int32)[:, None] * max_pages
        + jnp.arange(max_pages, dtype=jnp.int32)[None, :]
    )
    code = jnp.sum(jnp.where(matches, codes[None], 0), axis=(1, 2))
    slot_request = code // max_pages
    slot_page = code % max_pages
    slot_length = lookup(cache_lengths, slot_request, requests)
    begin = slot_page * PAGE_TOKENS
    live = is_held & (begin < slot_length + GROUP)
    fresh = live & (begin + PAGE_TOKENS > slot_length)
    flags = live.astype(jnp.int32) + fresh.astype(jnp.int32)

    def whole(*shape):
        return pl.BlockSpec(shape, lambda s, *_: (0,) * len(shape))

    def per_slot():
        return pl.BlockSpec((1, PAGE_TOKENS, width), lambda s, *_: (s, 0, 0))

    factor = math.log2(math.e) / math.sqrt(HEAD_SIZE)
    key_out, value_out, partial, stats = pl.pallas_call(
        functools.partial(attention_kernel, heads, factor),
        out_shape=(
            jax.ShapeDtypeStruct(key_cache.shape, BF16),
            jax.ShapeDtypeStruct(key_cache.shape, BF16),
            jax.ShapeDtypeStruct((pages, width, tok_dev), BF16),
            jax.ShapeDtypeStruct((pages, 16, tok_dev), F32),
        ),
        grid_spec=pltpu.PrefetchScalarGridSpec(
            num_scalar_prefetch=4,
            grid=(slots,),
            in_specs=[
                whole(every, width),
                whole(every, 2 * width),
                per_slot(),
                per_slot(),
            ],
            out_specs=(
                per_slot(),
                per_slot(),
                whole(pages, width, tok_dev),
                whole(pages, 16, tok_dev),
            ),
            scratch_shapes=[
                pltpu.VMEM((requests, width, GROUP), F32),
                pltpu.VMEM((requests, 8, GROUP), F32),
                pltpu.VMEM((requests, 8, GROUP), F32),
            ],
        ),
        compiler_params=pltpu.CompilerParams(
            dimension_semantics=("arbitrary",), vmem_limit_bytes=LIMIT
        ),
        name="attend_slots",
    )(slot_request, slot_page, slot_length, flags, q_all, kv_all, key_cache, paged_value_cache)

    new_hidden, next_qkv = pl.pallas_call(
        functools.partial(tail_kernel, heads),
        out_shape=(
            jax.ShapeDtypeStruct(hidden.shape, BF16),
            jax.ShapeDtypeStruct(group_qkv.shape, BF16),
        ),
        in_specs=[vmem, vmem, vmem, vmem, anywhere, vmem, vmem, vmem, anywhere, vmem],
        out_specs=(vmem, vmem),
        scratch_shapes=[
            pltpu.VMEM((pages, width, tok_dev), BF16),
            pltpu.VMEM((pages, 16, tok_dev), F32),
            pltpu.VMEM(dense_weight.shape, BF16),
            pltpu.VMEM(qkv_weight.shape, BF16),
            pltpu.VMEM((width, tok_dev), BF16),
            pltpu.VMEM((shares, tok_dev, share), BF16),
            pltpu.VMEM((shares, tok_dev, share), BF16),
            pltpu.VMEM((shares, tok_dev, share), BF16),
            pltpu.VMEM((tok_dev, share * shares), BF16),
            pltpu.VMEM((tok_dev, share), F32),
            dma((2,)),
            dma((pages,)),
            dma((pages,)),
            dma((pages,)),
            dma((pages,)),
            dma((shares,)),
            dma((shares,)),
            dma((shares,)),
            dma((shares,)),
        ],
        compiler_params=pltpu.CompilerParams(
            collective_id=1, has_side_effects=True, vmem_limit_bytes=LIMIT
        ),
        name="combine_project",
    )(
        partial, stats, hidden, mlp_branch, dense_weight, dense_bias[None, :], norm_gain[None, :],
        norm_bias[None, :], qkv_weight, qkv_bias[None, :],
    )
    return new_hidden, next_qkv, key_out, value_out


def solution(mesh):
    in_specs = (
        P("page", "head"), P("page", "head"), P("page", "head"),
        P("page", None, "head"), P("page", None, "head"),
        P(), P(), P("head", None), P(), P(), P(), P(None, "head"), P("head"),
    )
    out_specs = (
        P("page", "head"), P("page", "head"), P("page", None, "head"), P("page", None, "head"),
    )
    return jax.shard_map(
        on_device, mesh=mesh, in_specs=in_specs, out_specs=out_specs, check_vma=False
    )
```

```python
import functools
import math

import jax
import jax.numpy as jnp
from jax import lax
from jax.experimental import pallas as pl
from jax.experimental.pallas import tpu as pltpu
from jax.sharding import PartitionSpec as P

HEAD_SIZE = 128
ROT = 32
PAGE_TOKENS = 128
GROUP = 512
MESH = pl.DeviceIdType.MESH
FLOOR = -1e29
MASKED = -1e30
LIMIT = 56 * 1024 * 1024
BF16 = jnp.bfloat16
F32 = jnp.float32


def signal_all(axes):
    barrier = pltpu.get_barrier_semaphore()
    count = 0
    for axis in axes:
        size = lax.axis_size(axis)
        me = lax.axis_index(axis)
        for offset in range(1, size):
            pl.semaphore_signal(
                barrier,
                inc=1,
                device_id={axis: lax.rem(me + offset, size)},
                device_id_type=MESH,
            )
            count += 1
    return barrier, count


def gather_kernel(heads, x_ref, table_ref, q_ref, kv_ref, q_mine, kv_mine, send, recv, fsend, frecv, lsem):
    pages = lax.axis_size("page")
    chips = pages // 2
    me = lax.axis_index("page")
    chip = lax.div(me, 2)
    core = lax.rem(me, 2)
    sibling = chip * 2 + 1 - core
    rows = x_ref.shape[0]
    width = heads * HEAD_SIZE
    lane = lax.broadcasted_iota(jnp.int32, (rows, HEAD_SIZE), 1)
    barrier, count = signal_all(("page",))

    def rotated(column):
        x = x_ref[:, column : column + HEAD_SIZE].astype(F32)
        ahead = pltpu.roll(x, HEAD_SIZE - ROT // 2, 1)
        behind = pltpu.roll(x, ROT // 2, 1)
        other = jnp.where(lane < ROT // 2, ahead, behind)
        return (x * table_ref[0] + other * table_ref[1]).astype(BF16)

    for head in range(heads):
        base = head * 3 * HEAD_SIZE
        at = head * HEAD_SIZE
        q_mine[:, at : at + HEAD_SIZE] = rotated(base)
        kv_mine[:, at : at + HEAD_SIZE] = rotated(base + HEAD_SIZE)
        kv_mine[:, width + at : width + at + HEAD_SIZE] = x_ref[
            :, base + 2 * HEAD_SIZE : base + 3 * HEAD_SIZE
        ]

    pieces = (
        (q_mine, q_ref, slice(0, width)),
        (kv_mine, kv_ref, slice(0, width)),
        (kv_mine, kv_ref, slice(width, 2 * width)),
    )

    def source_of(piece):
        src, _, columns = pieces[piece]
        return src.at[:, columns]

    def block_of(piece, index, begin=0, size=rows):
        _, dst, columns = pieces[piece]
        return dst.at[pl.ds(pl.multiple_of(index * rows + begin, 16), size), columns]

    def push(src, dst, target, send_sem, recv_sem):
        copy = pltpu.make_async_remote_copy(
            src_ref=src,
            dst_ref=dst,
            send_sem=send_sem,
            recv_sem=recv_sem,
            device_id={"page": target},
            device_id_type=MESH,
        )
        copy.start()
        return copy

    local = []
    for which, (src, dst) in enumerate(((q_mine, q_ref), (kv_mine, kv_ref))):
        copy = pltpu.make_async_copy(
            src, dst.at[pl.ds(pl.multiple_of(me * rows, rows), rows), :], lsem.at[which]
        )
        copy.start()
        local.append(copy)
    pl.semaphore_wait(barrier, count)

    first, forwards = [], []

    def forward(piece, index, kind, begin=0, size=rows):
        landed = block_of(piece, index, begin, size)
        forwards.append(push(landed, landed, sibling, fsend.at[piece, kind], frecv.at[piece, kind]))

    span = range(len(pieces))
    if chips == 4:
        x = lax.rem(chip, 2)
        across = (chip + 1 - 2 * x) * 2 + core
        along = lax.rem(chip + 2, 4) * 2 + core
        corner = lax.rem(chip + 3 - 2 * x, 4) * 2 + core
        half = rows // 2
        from_across, from_along = [], []
        for piece in span:
            src, dst = source_of(piece), block_of(piece, me)
            from_across.append(push(src, dst, across, send.at[piece, 0], recv.at[piece, 0]))
            from_along.append(push(src, dst, along, send.at[piece, 1], recv.at[piece, 1]))
            forwards.append(push(src, dst, sibling, fsend.at[piece, 0], frecv.at[piece, 0]))
        low, high = [], []
        for piece in span:
            from_across[piece].wait_recv()
            landed = block_of(piece, across, 0, half)
            low.append(push(landed, landed, along, send.at[piece, 2], recv.at[piece, 2]))
            from_along[piece].wait_recv()
            landed = block_of(piece, along, half, half)
            high.append(push(landed, landed, across, send.at[piece, 3], recv.at[piece, 3]))
            forward(piece, across, 1)
            forward(piece, along, 2)
        for piece in span:
            low[piece].wait_recv()
            forward(piece, corner, 3, 0, half)
            high[piece].wait_recv()
            forward(piece, corner, 4, half, half)
        first = from_across + from_along + low + high
    else:
        for piece in span:
            src, dst = source_of(piece), block_of(piece, me)
            for offset in range(1, chips):
                target = lax.rem(chip + offset, chips) * 2 + core
                first.append(push(src, dst, target, send.at[piece, offset], recv.at[piece, offset]))
            forwards.append(push(src, dst, sibling, fsend.at[piece, 0], frecv.at[piece, 0]))
        for piece in span:
            for offset in range(1, chips):
                first[piece * (chips - 1) + offset - 1].wait_recv()
                forward(piece, lax.rem(chip + chips - offset, chips) * 2 + core, offset)
    for copy in local:
        copy.wait()
    for copy in first:
        copy.wait_send()
    for copy in forwards:
        copy.wait()


def attention_kernel(
    heads, factor,
    len_ref, table_ref, q_hbm, kv_hbm, kc_hbm, vc_hbm,
    ko_hbm, vo_hbm, o_ref, st_ref,
    q_ref, kv_ref, keys, values, acc, m_s, l_s, code, in_sem, out_sem, q_sem,
):
    requests, max_pages = table_ref.shape
    slots = keys.shape[0]
    width = heads * HEAD_SIZE
    tok_dev = o_ref.shape[2]
    base = lax.axis_index("page") * slots

    load_q = pltpu.make_async_copy(q_hbm, q_ref, q_sem.at[0])
    load_kv = pltpu.make_async_copy(kv_hbm, kv_ref, q_sem.at[1])
    load_q.start()

    def page_in(slot):
        return (
            pltpu.make_async_copy(kc_hbm.at[slot], keys.at[slot], in_sem.at[0, slot]),
            pltpu.make_async_copy(vc_hbm.at[slot], values.at[slot], in_sem.at[1, slot]),
        )

    def page_out(slot):
        return (
            pltpu.make_async_copy(keys.at[slot], ko_hbm.at[slot], out_sem.at[0, slot]),
            pltpu.make_async_copy(values.at[slot], vo_hbm.at[slot], out_sem.at[1, slot]),
        )

    for slot in range(slots):
        for copy in page_in(slot):
            copy.start()
        if slot == 0:
            load_kv.start()
    for slot in range(slots + 1):
        code[slot] = 0
    for r in range(requests):

        def place(i, _):
            slot = table_ref[r, i] - base
            held = (slot >= 0) & (slot < slots)
            code[jnp.where(held, slot, slots)] = r * max_pages + i + 1
            return 0

        lax.fori_loop(0, max_pages, place, 0)
    acc[...] = jnp.zeros_like(acc)
    m_s[...] = jnp.full_like(m_s, FLOOR)
    l_s[...] = jnp.zeros_like(l_s)
    load_q.wait()
    load_kv.wait()

    def attend(slot, request, start, masked):
        mine = pl.ds(pl.multiple_of(request * GROUP, GROUP), GROUP)
        for head in range(heads):
            at = slice(head * HEAD_SIZE, (head + 1) * HEAD_SIZE)
            scores = (
                lax.dot_general(
                    keys[slot, :, at], q_ref[mine, at], (((1,), (1,)), ((), ())),
                    preferred_element_type=F32,
                )
                * factor
            )
            if masked:
                row = start + lax.broadcasted_iota(jnp.int32, scores.shape, 0)
                column = lax.broadcasted_iota(jnp.int32, scores.shape, 1)
                scores = jnp.where(row <= column, scores, MASKED)
            m_old = m_s[request, head : head + 1, :]
            m_new = jnp.maximum(m_old, jnp.max(scores, axis=0, keepdims=True))
            fade = jnp.exp2(m_old - m_new)
            weights = jnp.exp2(scores - m_new)
            m_s[request, head : head + 1, :] = m_new
            l_s[request, head : head + 1, :] = l_s[request, head : head + 1, :] * fade + jnp.sum(
                weights, axis=0, keepdims=True
            )
            part = lax.dot_general(
                values[slot, :, at], weights.astype(BF16), (((0,), (0,)), ((), ())),
                preferred_element_type=F32,
            )
            acc[request, at, :] = acc[request, at, :] * fade + part

    def step(slot, _):
        for copy in page_in(slot):
            copy.wait()
        known = code[slot]
        entry = jnp.maximum(known - 1, 0)
        request = lax.div(entry, max_pages)
        start = lax.rem(entry, max_pages) * PAGE_TOKENS - len_ref[request]
        live = (known > 0) & (start < GROUP)
        old = live & (start <= -PAGE_TOKENS)
        new = live & (start > -PAGE_TOKENS)

        @pl.when(new)
        def _():
            mine = pl.ds(pl.multiple_of(request * GROUP, GROUP), GROUP)
            row = start + lax.broadcasted_iota(jnp.int32, (PAGE_TOKENS, GROUP), 0)
            column = lax.broadcasted_iota(jnp.int32, (PAGE_TOKENS, GROUP), 1)
            pick = jnp.where(row == column, 1.0, 0.0).astype(BF16)
            place = start + lax.broadcasted_iota(jnp.int32, (PAGE_TOKENS, width), 0)
            fresh = (place >= 0) & (place < GROUP)
            for part, held in enumerate((keys, values)):
                moved = jnp.dot(
                    pick, kv_ref[mine, part * width : (part + 1) * width], preferred_element_type=F32
                )
                held[slot] = jnp.where(fresh, moved, held[slot].astype(F32)).astype(BF16)

        for copy in page_out(slot):
            copy.start()
        pl.when(old)(lambda: attend(slot, request, start, False))
        pl.when(new)(lambda: attend(slot, request, start, True))
        return 0

    lax.fori_loop(0, slots, step, 0)

    per = GROUP // tok_dev
    for r in range(requests):
        for b in range(per):
            columns = slice(b * tok_dev, (b + 1) * tok_dev)
            o_ref[r * per + b] = acc[r, :, columns].astype(BF16)
            st_ref[r * per + b, 0:8, :] = m_s[r, :, columns]
            st_ref[r * per + b, 8:16, :] = l_s[r, :, columns]

    def drain(slot, _):
        for copy in page_out(slot):
            copy.wait()
        return 0

    lax.fori_loop(0, slots, drain, 0)


def tail_kernel(
    heads,
    o_ref, st_ref, hidden_ref, branch_ref, dw_ref, dbias_ref, gain_ref, nbias_ref, qw_ref, qbias_ref,
    hid_out, qkv_out,
    o_in, st_in, dw, qw, att, proj, proj_in, stream, normed, total,
    wsem, osend, orecv, ssend, srecv, psend, precv, gsend, grecv,
):
    pages = lax.axis_size("page")
    shares = lax.axis_size("head")
    me = lax.axis_index("page")
    mz = lax.axis_index("head")
    share = hidden_ref.shape[1]
    model = share * shares

    load_dw = pltpu.make_async_copy(dw_ref, dw, wsem.at[0])
    load_qw = pltpu.make_async_copy(qw_ref, qw, wsem.at[1])
    load_dw.start()
    barrier, count = signal_all(("page", "head"))
    pl.semaphore_wait(barrier, count)

    copies = []
    for offset in range(1, pages):
        target = lax.rem(me + offset, pages)
        for src, dst, ss, rs in ((st_ref, st_in, ssend, srecv), (o_ref, o_in, osend, orecv)):
            copy = pltpu.make_async_remote_copy(
                src_ref=src.at[target],
                dst_ref=dst.at[offset],
                send_sem=ss.at[offset],
                recv_sem=rs.at[offset],
                device_id={"page": target},
                device_id_type=MESH,
            )
            copy.start()
            copies.append(copy)
    load_qw.start()
    st_in[0] = st_ref[me]
    o_in[0] = o_ref[me]
    for copy in copies:
        copy.wait()

    def combine(head):
        rows = pl.ds(pl.multiple_of(head * HEAD_SIZE, HEAD_SIZE), HEAD_SIZE)

        def raise_peak(j, peak):
            return jnp.maximum(peak, st_in[j, pl.ds(head, 1), :])

        peak = lax.fori_loop(0, pages, raise_peak, jnp.full((1, o_in.shape[2]), FLOOR, F32))

        def add(j, pair):
            summed, count = pair
            scale = jnp.exp2(st_in[j, pl.ds(head, 1), :] - peak)
            return (
                summed + o_in[j, rows, :].astype(F32) * scale,
                count + st_in[j, pl.ds(8 + head, 1), :] * scale,
            )

        summed, count = lax.fori_loop(
            0,
            pages,
            add,
            (jnp.zeros((HEAD_SIZE, o_in.shape[2]), F32), jnp.zeros((1, o_in.shape[2]), F32)),
        )
        att[rows, :] = (summed / count).astype(BF16)

    for head in range(heads):
        combine(head)
    load_dw.wait()

    def project(share_index):
        columns = pl.ds(pl.multiple_of(share_index * share, share), share)
        return lax.dot_general(
            att[...], dw[:, columns], (((0,), (0,)), ((), ())), preferred_element_type=F32
        )

    sums = []
    for offset in range(1, shares):
        target = lax.rem(mz + offset, shares)
        proj[offset] = project(target).astype(BF16)
        copy = pltpu.make_async_remote_copy(
            src_ref=proj.at[offset],
            dst_ref=proj_in.at[offset],
            send_sem=psend.at[offset],
            recv_sem=precv.at[offset],
            device_id={"head": target},
            device_id_type=MESH,
        )
        copy.start()
        sums.append(copy)
    my_columns = pl.ds(pl.multiple_of(mz * share, share), share)
    total[...] = (
        project(mz)
        + dbias_ref[:, my_columns]
        + hidden_ref[...].astype(F32)
        + branch_ref[...].astype(F32)
    )
    for offset in range(1, shares):
        sums[offset - 1].wait()
        total[...] += proj_in[offset].astype(F32)
    mine = total[...].astype(BF16)
    hid_out[...] = mine
    stream[mz] = mine
    gathers = []
    for offset in range(1, shares):
        copy = pltpu.make_async_remote_copy(
            src_ref=hid_out,
            dst_ref=stream.at[mz],
            send_sem=gsend.at[offset],
            recv_sem=grecv.at[offset],
            device_id={"head": lax.rem(mz + offset, shares)},
            device_id_type=MESH,
        )
        copy.start()
        gathers.append(copy)
    load_qw.wait()
    for copy in gathers:
        copy.wait()

    rows = hidden_ref.shape[0]

    def moments(j, pair):
        x = stream[j].astype(F32)
        return (
            pair[0] + jnp.sum(x, axis=1, keepdims=True),
            pair[1] + jnp.sum(x * x, axis=1, keepdims=True),
        )

    first, second = lax.fori_loop(
        0, shares, moments, (jnp.zeros((rows, 1), F32), jnp.zeros((rows, 1), F32))
    )
    mean = first / model
    scale = lax.rsqrt(second / model - mean * mean + 1e-05)
    for j in range(shares):
        columns = slice(j * share, (j + 1) * share)
        x = stream[j].astype(F32)
        normed[:, columns] = ((x - mean) * scale * gain_ref[:, columns] + nbias_ref[:, columns]).astype(BF16)

    block = 256
    for j in range(qkv_out.shape[1] // block):
        columns = slice(j * block, (j + 1) * block)
        out = jnp.dot(normed[...], qw[:, columns], preferred_element_type=F32)
        qkv_out[:, columns] = (out + qbias_ref[:, columns]).astype(BF16)


def lookup(table_values, index_rows, count_all):
    matched = index_rows[..., None] == jnp.arange(count_all, dtype=jnp.int32)
    return jnp.sum(jnp.where(matched, table_values, 0), axis=-1)


def on_device(
    hidden, group_qkv, mlp_branch, key_cache, paged_value_cache, cache_lengths, page_table,
    dense_weight, dense_bias, norm_gain, norm_bias, qkv_weight, qkv_bias,
):
    tok_dev, share = hidden.shape
    pages = lax.axis_size("page")
    shares = lax.axis_size("head")
    me = lax.axis_index("page")
    requests = cache_lengths.shape[0]
    slots = key_cache.shape[0]
    heads = group_qkv.shape[1] // (3 * HEAD_SIZE)
    width = heads * HEAD_SIZE
    every = tok_dev * pages
    vmem = pl.BlockSpec(memory_space=pltpu.VMEM)
    anywhere = pl.BlockSpec(memory_space=pl.ANY)
    dma = pltpu.SemaphoreType.DMA

    global_rows = me * tok_dev + jnp.arange(tok_dev, dtype=jnp.int32)
    positions = lookup(cache_lengths, global_rows // GROUP, requests) + global_rows % GROUP
    lane = jnp.arange(HEAD_SIZE, dtype=jnp.int32)
    half = ROT // 2
    inverse = 1.0 / 10000.0 ** ((2 * (lane % half)).astype(F32) / ROT)
    angles = positions.astype(F32)[:, None] * inverse[None, :]
    turned = lane[None, :] < ROT
    sine = jnp.sin(angles)
    table = jnp.stack(
        [
            jnp.where(turned, jnp.cos(angles), 1.0),
            jnp.where(turned, jnp.where(lane[None, :] < half, -sine, sine), 0.0),
        ]
    )

    q_all, kv_all = pl.pallas_call(
        functools.partial(gather_kernel, heads),
        out_shape=(
            jax.ShapeDtypeStruct((every, width), BF16),
            jax.ShapeDtypeStruct((every, 2 * width), BF16),
        ),
        in_specs=[vmem, vmem],
        out_specs=(anywhere, anywhere),
        scratch_shapes=[
            pltpu.VMEM((tok_dev, width), BF16),
            pltpu.VMEM((tok_dev, 2 * width), BF16),
            dma((3, max(4, pages // 2))),
            dma((3, max(4, pages // 2))),
            dma((3, max(5, pages // 2))),
            dma((3, max(5, pages // 2))),
            dma((2,)),
        ],
        compiler_params=pltpu.CompilerParams(
            collective_id=0, has_side_effects=True, vmem_limit_bytes=LIMIT
        ),
        name="gather_qkv",
    )(group_qkv, table)

    factor = math.log2(math.e) / math.sqrt(HEAD_SIZE)
    smem = pl.BlockSpec(memory_space=pltpu.SMEM)
    key_out, value_out, partial, stats = pl.pallas_call(
        functools.partial(attention_kernel, heads, factor),
        out_shape=(
            jax.ShapeDtypeStruct(key_cache.shape, BF16),
            jax.ShapeDtypeStruct(key_cache.shape, BF16),
            jax.ShapeDtypeStruct((pages, width, tok_dev), BF16),
            jax.ShapeDtypeStruct((pages, 16, tok_dev), F32),
        ),
        in_specs=[smem, smem, anywhere, anywhere, anywhere, anywhere],
        out_specs=(anywhere, anywhere, vmem, vmem),
        scratch_shapes=[
            pltpu.VMEM((every, width), BF16),
            pltpu.VMEM((every, 2 * width), BF16),
            pltpu.VMEM(key_cache.shape, BF16),
            pltpu.VMEM(key_cache.shape, BF16),
            pltpu.VMEM((requests, width, GROUP), F32),
            pltpu.VMEM((requests, 8, GROUP), F32),
            pltpu.VMEM((requests, 8, GROUP), F32),
            pltpu.SMEM((slots + 1,), jnp.int32),
            dma((2, slots)),
            dma((2, slots)),
            dma((2,)),
        ],
        compiler_params=pltpu.CompilerParams(vmem_limit_bytes=LIMIT),
        name="attend_slots",
    )(cache_lengths, page_table, q_all, kv_all, key_cache, paged_value_cache)

    new_hidden, next_qkv = pl.pallas_call(
        functools.partial(tail_kernel, heads),
        out_shape=(
            jax.ShapeDtypeStruct(hidden.shape, BF16),
            jax.ShapeDtypeStruct(group_qkv.shape, BF16),
        ),
        in_specs=[vmem, vmem, vmem, vmem, anywhere, vmem, vmem, vmem, anywhere, vmem],
        out_specs=(vmem, vmem),
        scratch_shapes=[
            pltpu.VMEM((pages, width, tok_dev), BF16),
            pltpu.VMEM((pages, 16, tok_dev), F32),
            pltpu.VMEM(dense_weight.shape, BF16),
            pltpu.VMEM(qkv_weight.shape, BF16),
            pltpu.VMEM((width, tok_dev), BF16),
            pltpu.VMEM((shares, tok_dev, share), BF16),
            pltpu.VMEM((shares, tok_dev, share), BF16),
            pltpu.VMEM((shares, tok_dev, share), BF16),
            pltpu.VMEM((tok_dev, share * shares), BF16),
            pltpu.VMEM((tok_dev, share), F32),
            dma((2,)),
            dma((pages,)),
            dma((pages,)),
            dma((pages,)),
            dma((pages,)),
            dma((shares,)),
            dma((shares,)),
            dma((shares,)),
            dma((shares,)),
        ],
        compiler_params=pltpu.CompilerParams(
            collective_id=1, has_side_effects=True, vmem_limit_bytes=LIMIT
        ),
        name="combine_project",
    )(
        partial, stats, hidden, mlp_branch, dense_weight, dense_bias[None, :], norm_gain[None, :],
        norm_bias[None, :], qkv_weight, qkv_bias[None, :],
    )
    return new_hidden, next_qkv, key_out, value_out


def solution(mesh):
    in_specs = (
        P("page", "head"), P("page", "head"), P("page", "head"),
        P("page", None, "head"), P("page", None, "head"),
        P(), P(), P("head", None), P(), P(), P(), P(None, "head"), P("head"),
    )
    out_specs = (
        P("page", "head"), P("page", "head"), P("page", None, "head"), P("page", None, "head"),
    )
    return jax.shard_map(
        on_device, mesh=mesh, in_specs=in_specs, out_specs=out_specs, check_vma=False
    )
```

```python
import functools
import math

import jax
import jax.numpy as jnp
from jax import lax
from jax.experimental import pallas as pl
from jax.experimental.pallas import tpu as pltpu
from jax.sharding import PartitionSpec as P

HEAD_SIZE = 128
ROT = 32
PAGE_TOKENS = 128
GROUP = 512
MESH = pl.DeviceIdType.MESH
FLOOR = -1e29
MASKED = -1e30
LIMIT = 56 * 1024 * 1024
BF16 = jnp.bfloat16
F32 = jnp.float32


def signal_all(axes):
    barrier = pltpu.get_barrier_semaphore()
    count = 0
    for axis in axes:
        size = lax.axis_size(axis)
        me = lax.axis_index(axis)
        for offset in range(1, size):
            pl.semaphore_signal(
                barrier,
                inc=1,
                device_id={axis: lax.rem(me + offset, size)},
                device_id_type=MESH,
            )
            count += 1
    return barrier, count


def gather_kernel(heads, x_ref, table_ref, q_ref, kv_ref, q_mine, kv_mine, send, recv, fsend, frecv, lsem):
    pages = lax.axis_size("page")
    chips = pages // 2
    me = lax.axis_index("page")
    chip = lax.div(me, 2)
    core = lax.rem(me, 2)
    sibling = chip * 2 + 1 - core
    rows = x_ref.shape[0]
    width = heads * HEAD_SIZE
    lane = lax.broadcasted_iota(jnp.int32, (rows, HEAD_SIZE), 1)
    barrier, count = signal_all(("page",))

    def rotated(column):
        x = x_ref[:, column : column + HEAD_SIZE].astype(F32)
        ahead = pltpu.roll(x, HEAD_SIZE - ROT // 2, 1)
        behind = pltpu.roll(x, ROT // 2, 1)
        other = jnp.where(lane < ROT // 2, ahead, behind)
        return (x * table_ref[0] + other * table_ref[1]).astype(BF16)

    for head in range(heads):
        base = head * 3 * HEAD_SIZE
        at = head * HEAD_SIZE
        q_mine[:, at : at + HEAD_SIZE] = rotated(base)
        kv_mine[:, at : at + HEAD_SIZE] = rotated(base + HEAD_SIZE)
        kv_mine[:, width + at : width + at + HEAD_SIZE] = x_ref[
            :, base + 2 * HEAD_SIZE : base + 3 * HEAD_SIZE
        ]

    pieces = (
        (q_mine, q_ref, slice(0, width)),
        (kv_mine, kv_ref, slice(0, width)),
        (kv_mine, kv_ref, slice(width, 2 * width)),
    )

    def source_of(piece):
        src, _, columns = pieces[piece]
        return src.at[:, columns]

    def block_of(piece, index, begin=0, size=rows):
        _, dst, columns = pieces[piece]
        return dst.at[pl.ds(pl.multiple_of(index * rows + begin, 16), size), columns]

    def push(src, dst, target, send_sem, recv_sem):
        copy = pltpu.make_async_remote_copy(
            src_ref=src,
            dst_ref=dst,
            send_sem=send_sem,
            recv_sem=recv_sem,
            device_id={"page": target},
            device_id_type=MESH,
        )
        copy.start()
        return copy

    local = []
    for which, (src, dst) in enumerate(((q_mine, q_ref), (kv_mine, kv_ref))):
        copy = pltpu.make_async_copy(
            src, dst.at[pl.ds(pl.multiple_of(me * rows, rows), rows), :], lsem.at[which]
        )
        copy.start()
        local.append(copy)
    pl.semaphore_wait(barrier, count)

    first, forwards = [], []

    def forward(piece, index, kind, begin=0, size=rows):
        landed = block_of(piece, index, begin, size)
        forwards.append(push(landed, landed, sibling, fsend.at[piece, kind], frecv.at[piece, kind]))

    span = range(len(pieces))
    if chips == 4:
        x = lax.rem(chip, 2)
        across = (chip + 1 - 2 * x) * 2 + core
        along = lax.rem(chip + 2, 4) * 2 + core
        corner = lax.rem(chip + 3 - 2 * x, 4) * 2 + core
        half = rows // 2
        from_across, from_along = [], []
        for piece in span:
            src, dst = source_of(piece), block_of(piece, me)
            from_across.append(push(src, dst, across, send.at[piece, 0], recv.at[piece, 0]))
            from_along.append(push(src, dst, along, send.at[piece, 1], recv.at[piece, 1]))
            forwards.append(push(src, dst, sibling, fsend.at[piece, 0], frecv.at[piece, 0]))
        low, high = [], []
        for piece in span:
            from_across[piece].wait_recv()
            landed = block_of(piece, across, 0, half)
            low.append(push(landed, landed, along, send.at[piece, 2], recv.at[piece, 2]))
            from_along[piece].wait_recv()
            landed = block_of(piece, along, half, half)
            high.append(push(landed, landed, across, send.at[piece, 3], recv.at[piece, 3]))
            forward(piece, across, 1)
            forward(piece, along, 2)
        for piece in span:
            low[piece].wait_recv()
            forward(piece, corner, 3, 0, half)
            high[piece].wait_recv()
            forward(piece, corner, 4, half, half)
        first = from_across + from_along + low + high
    else:
        for piece in span:
            src, dst = source_of(piece), block_of(piece, me)
            for offset in range(1, chips):
                target = lax.rem(chip + offset, chips) * 2 + core
                first.append(push(src, dst, target, send.at[piece, offset], recv.at[piece, offset]))
            forwards.append(push(src, dst, sibling, fsend.at[piece, 0], frecv.at[piece, 0]))
        for piece in span:
            for offset in range(1, chips):
                first[piece * (chips - 1) + offset - 1].wait_recv()
                forward(piece, lax.rem(chip + chips - offset, chips) * 2 + core, offset)
    for copy in local:
        copy.wait()
    for copy in first:
        copy.wait_send()
    for copy in forwards:
        copy.wait()


def attention_kernel(
    heads, factor,
    len_ref, table_ref, q_hbm, kv_hbm, kc_hbm, vc_hbm,
    ko_hbm, vo_hbm, o_ref, st_ref,
    q_ref, kv_ref, keys, values, acc, m_s, l_s, code, in_sem, out_sem, q_sem,
):
    requests, max_pages = table_ref.shape
    slots = keys.shape[0]
    width = heads * HEAD_SIZE
    tok_dev = o_ref.shape[2]
    base = lax.axis_index("page") * slots

    load_q = pltpu.make_async_copy(q_hbm, q_ref, q_sem.at[0])
    load_kv = pltpu.make_async_copy(kv_hbm, kv_ref, q_sem.at[1])
    load_q.start()

    def page_in(slot):
        return (
            pltpu.make_async_copy(kc_hbm.at[slot], keys.at[slot], in_sem.at[0, slot]),
            pltpu.make_async_copy(vc_hbm.at[slot], values.at[slot], in_sem.at[1, slot]),
        )

    def page_out(slot):
        return (
            pltpu.make_async_copy(keys.at[slot], ko_hbm.at[slot], out_sem.at[0, slot]),
            pltpu.make_async_copy(values.at[slot], vo_hbm.at[slot], out_sem.at[1, slot]),
        )

    for slot in range(slots):
        for copy in page_in(slot):
            copy.start()
        if slot == 0:
            load_kv.start()
    for slot in range(slots + 1):
        code[slot] = 0
    for r in range(requests):

        def place(i, _):
            slot = table_ref[r, i] - base
            held = (slot >= 0) & (slot < slots)
            code[jnp.where(held, slot, slots)] = r * max_pages + i + 1
            return 0

        lax.fori_loop(0, max_pages, place, 0)
    acc[...] = jnp.zeros_like(acc)
    m_s[...] = jnp.full_like(m_s, FLOOR)
    l_s[...] = jnp.zeros_like(l_s)
    load_q.wait()
    load_kv.wait()

    def attend(slot, request, start, masked):
        mine = pl.ds(pl.multiple_of(request * GROUP, GROUP), GROUP)
        for head in range(heads):
            at = slice(head * HEAD_SIZE, (head + 1) * HEAD_SIZE)
            scores = (
                lax.dot_general(
                    keys[slot, :, at], q_ref[mine, at], (((1,), (1,)), ((), ())),
                    preferred_element_type=F32,
                )
                * factor
            )
            if masked:
                row = start + lax.broadcasted_iota(jnp.int32, scores.shape, 0)
                column = lax.broadcasted_iota(jnp.int32, scores.shape, 1)
                scores = jnp.where(row <= column, scores, MASKED)
            m_old = m_s[request, head : head + 1, :]
            m_new = jnp.maximum(m_old, jnp.max(scores, axis=0, keepdims=True))
            fade = jnp.exp2(m_old - m_new)
            weights = jnp.exp2(scores - m_new)
            m_s[request, head : head + 1, :] = m_new
            l_s[request, head : head + 1, :] = l_s[request, head : head + 1, :] * fade + jnp.sum(
                weights, axis=0, keepdims=True
            )
            part = lax.dot_general(
                values[slot, :, at], weights.astype(BF16), (((0,), (0,)), ((), ())),
                preferred_element_type=F32,
            )
            acc[request, at, :] = acc[request, at, :] * fade + part

    def step(slot, _):
        for copy in page_in(slot):
            copy.wait()
        known = code[slot]
        entry = jnp.maximum(known - 1, 0)
        request = lax.div(entry, max_pages)
        start = lax.rem(entry, max_pages) * PAGE_TOKENS - len_ref[request]
        live = (known > 0) & (start < GROUP)
        old = live & (start <= -PAGE_TOKENS)
        new = live & (start > -PAGE_TOKENS)

        @pl.when(new)
        def _():
            mine = pl.ds(pl.multiple_of(request * GROUP, GROUP), GROUP)
            row = start + lax.broadcasted_iota(jnp.int32, (PAGE_TOKENS, GROUP), 0)
            column = lax.broadcasted_iota(jnp.int32, (PAGE_TOKENS, GROUP), 1)
            pick = jnp.where(row == column, 1.0, 0.0).astype(BF16)
            place = start + lax.broadcasted_iota(jnp.int32, (PAGE_TOKENS, width), 0)
            fresh = (place >= 0) & (place < GROUP)
            for part, held in enumerate((keys, values)):
                moved = jnp.dot(
                    pick, kv_ref[mine, part * width : (part + 1) * width], preferred_element_type=F32
                )
                held[slot] = jnp.where(fresh, moved, held[slot].astype(F32)).astype(BF16)

        for copy in page_out(slot):
            copy.start()
        pl.when(old)(lambda: attend(slot, request, start, False))
        pl.when(new)(lambda: attend(slot, request, start, True))
        return 0

    lax.fori_loop(0, slots, step, 0)

    per = GROUP // tok_dev
    for r in range(requests):
        for b in range(per):
            columns = slice(b * tok_dev, (b + 1) * tok_dev)
            o_ref[r * per + b] = acc[r, :, columns].astype(BF16)
            st_ref[r * per + b, 0:8, :] = m_s[r, :, columns]
            st_ref[r * per + b, 8:16, :] = l_s[r, :, columns]

    def drain(slot, _):
        for copy in page_out(slot):
            copy.wait()
        return 0

    lax.fori_loop(0, slots, drain, 0)


def tail_kernel(
    heads, chunks,
    o_ref, st_ref, hidden_ref, branch_ref, dw_ref, dbias_ref, gain_ref, nbias_ref, qw_ref, qbias_ref,
    hid_out, qkv_out,
    o_sib, st_sib, o_pair, st_pair, o_in, st_in, dw, qw, att, proj,
    right_in, right_out, left_in, left_out, stream, normed, total,
    wsem, bsend, brecv, osend, orecv,
    rsend, rrecv, lsend, lrecv, grsend, grrecv, glsend, glrecv,
):
    pages = lax.axis_size("page")
    chips = pages // 2
    shares = lax.axis_size("head")
    me = lax.axis_index("page")
    mz = lax.axis_index("head")
    chip = lax.div(me, 2)
    core = lax.rem(me, 2)
    rows, share = hidden_ref.shape
    model = share * shares
    piece = rows // chunks

    load_dw = pltpu.make_async_copy(dw_ref, dw, wsem.at[0])
    load_qw = pltpu.make_async_copy(qw_ref, qw, wsem.at[1])
    load_dw.start()
    barrier, count = signal_all(("page", "head"))
    pl.semaphore_wait(barrier, count)

    def page_push(src, dst, target, send_sem, recv_sem):
        copy = pltpu.make_async_remote_copy(
            src_ref=src,
            dst_ref=dst,
            send_sem=send_sem,
            recv_sem=recv_sem,
            device_id={"page": target},
            device_id_type=MESH,
        )
        copy.start()
        return copy

    order = list(range(chips - 1, 0, -1)) + [0]
    shared = {}
    for k in order:
        theirs = lax.rem(chip + k, chips) * 2 + 1 - core
        shared[k] = (
            page_push(st_ref.at[theirs], st_sib.at[k], chip * 2 + 1 - core, bsend.at[0, k], brecv.at[0, k]),
            page_push(o_ref.at[theirs], o_sib.at[k], chip * 2 + 1 - core, bsend.at[1, k], brecv.at[1, k]),
        )
    load_qw.start()
    sent = []
    for k in order:
        for copy in shared[k]:
            copy.wait()
        ours = lax.rem(chip + k, chips) * 2 + core
        for head in range(heads):
            at = slice(head * HEAD_SIZE, (head + 1) * HEAD_SIZE)
            m_mine = st_ref[ours, head : head + 1, :]
            m_sib = st_sib[k, head : head + 1, :]
            peak = jnp.maximum(m_mine, m_sib)
            e_mine = jnp.exp2(m_mine - peak)
            e_sib = jnp.exp2(m_sib - peak)
            st_pair[k, head : head + 1, :] = peak
            st_pair[k, 8 + head : 9 + head, :] = (
                st_ref[ours, 8 + head : 9 + head, :] * e_mine + st_sib[k, 8 + head : 9 + head, :] * e_sib
            )
            o_pair[k, at, :] = (
                o_ref[ours, at, :].astype(F32) * e_mine + o_sib[k, at, :].astype(F32) * e_sib
            ).astype(BF16)
        if k:
            sent.append(page_push(st_pair.at[k], st_in.at[k], ours, osend.at[0, k], orecv.at[0, k]))
            sent.append(page_push(o_pair.at[k], o_in.at[k], ours, osend.at[1, k], orecv.at[1, k]))
    st_in[0] = st_pair[0]
    o_in[0] = o_pair[0]
    total[...] = dbias_ref[:, pl.ds(pl.multiple_of(mz * share, share), share)] + (
        hidden_ref[...].astype(F32) + branch_ref[...].astype(F32)
    )
    for copy in sent:
        copy.wait()

    for head in range(heads):
        at = slice(head * HEAD_SIZE, (head + 1) * HEAD_SIZE)

        def raise_peak(j, peak):
            return jnp.maximum(peak, st_in[j, head : head + 1, :])

        peak = lax.fori_loop(1, chips, raise_peak, st_in[0, head : head + 1, :])

        def add(j, pair):
            summed, count = pair
            scale = jnp.exp2(st_in[j, head : head + 1, :] - peak)
            return (
                summed + o_in[j, at, :].astype(F32) * scale,
                count + st_in[j, 8 + head : 9 + head, :] * scale,
            )

        summed, count = lax.fori_loop(
            0, chips, add, (jnp.zeros((HEAD_SIZE, rows), F32), jnp.zeros((1, rows), F32))
        )
        att[:, at] = (summed / count).T.astype(BF16)
    load_dw.wait()
    for t in range(shares):
        columns = slice(t * share, (t + 1) * share)
        part = jnp.dot(att[...], dw[:, columns], preferred_element_type=F32)
        proj[t] = part.astype(BF16)

        @pl.when(mz == t)
        def _():
            total[...] += part

    def part_of(ref, t, c):
        return ref.at[t, pl.ds(c * piece, piece), :]

    def z_copy(src, dst, send_sem, recv_sem, c, t, step):
        return pltpu.make_async_remote_copy(
            src_ref=part_of(src, t, c),
            dst_ref=part_of(dst, t, c),
            send_sem=send_sem.at[c, t],
            recv_sem=recv_sem.at[c, t],
            device_id={"head": jnp.clip(mz + step, 0, shares - 1)},
            device_id_type=MESH,
        )

    def right_copy(c, t):
        return z_copy(right_out, right_in, rsend, rrecv, c, t, 1)

    def left_copy(c, t):
        return z_copy(left_out, left_in, lsend, lrecv, c, t, -1)

    def gather_right(c, t):
        return z_copy(stream, stream, grsend, grrecv, c, t, 1)

    def gather_left(c, t):
        return z_copy(stream, stream, glsend, glrecv, c, t, -1)

    last = shares - 1

    def pass_on(c, t, sends, receives, copy, landed, out):
        at = slice(c * piece, (c + 1) * piece)

        @pl.when(sends & receives)
        def _():
            copy(c, t).wait_recv()
            out[t, at, :] = (proj[t, at, :].astype(F32) + landed[t, at, :].astype(F32)).astype(BF16)
            copy(c, t).start()

        @pl.when(sends & jnp.logical_not(receives))
        def _():
            out[t, at, :] = proj[t, at, :]
            copy(c, t).start()

    def sum_chunk(c):
        for i in range(last):
            pass_on(c, last - i, mz < last - i, mz > 0, right_copy, right_in, right_out)
            pass_on(c, i, mz > i, mz < last, left_copy, left_in, left_out)

    def finish_chunk(c):
        at = slice(c * piece, (c + 1) * piece)

        @pl.when(mz > 0)
        def _():
            right_copy(c, mz).wait_recv()
            total[at, :] += right_in[mz, at, :].astype(F32)

        @pl.when(mz < last)
        def _():
            left_copy(c, mz).wait_recv()
            total[at, :] += left_in[mz, at, :].astype(F32)

        mine = total[at, :].astype(BF16)
        hid_out[at, :] = mine
        stream[mz, at, :] = mine
        pl.when(mz < last)(lambda: gather_right(c, mz).start())
        pl.when(mz > 0)(lambda: gather_left(c, mz).start())

    def relay_chunk(c):
        for i in range(last):
            near, far = last - 1 - i, i + 1

            @pl.when(mz > near)
            def _():
                gather_right(c, near).wait_recv()
                pl.when(mz < last)(lambda: gather_right(c, near).start())

            @pl.when(mz < far)
            def _():
                gather_left(c, far).wait_recv()
                pl.when(mz > 0)(lambda: gather_left(c, far).start())

    def norm_chunk(c):
        at = slice(c * piece, (c + 1) * piece)
        first = jnp.zeros((piece, 1), F32)
        second = jnp.zeros((piece, 1), F32)
        for j in range(shares):
            x = stream[j, at, :].astype(F32)
            first += jnp.sum(x, axis=1, keepdims=True)
            second += jnp.sum(x * x, axis=1, keepdims=True)
        mean = first / model
        scale = lax.rsqrt(second / model - mean * mean + 1e-05)
        for j in range(shares):
            columns = slice(j * share, (j + 1) * share)
            x = stream[j, at, :].astype(F32)
            normed[at, columns] = (
                (x - mean) * scale * gain_ref[:, columns] + nbias_ref[:, columns]
            ).astype(BF16)

    sum_chunk(0)
    for c in range(chunks):
        if c + 1 < chunks:
            sum_chunk(c + 1)
        finish_chunk(c)
        if c:
            relay_chunk(c - 1)
            if c > 1:
                norm_chunk(c - 2)
    relay_chunk(chunks - 1)
    load_qw.wait()
    for c in range(max(chunks - 2, 0), chunks):
        norm_chunk(c)

    block = 256
    for j in range(qkv_out.shape[1] // block):
        columns = slice(j * block, (j + 1) * block)
        out = jnp.dot(normed[...], qw[:, columns], preferred_element_type=F32)
        qkv_out[:, columns] = (out + qbias_ref[:, columns]).astype(BF16)

    for c in range(chunks):
        for t in range(shares):
            pl.when(mz < t)(lambda: right_copy(c, t).wait_send())
            pl.when(mz > t)(lambda: left_copy(c, t).wait_send())
            pl.when((mz >= t) & (mz < last))(lambda: gather_right(c, t).wait_send())
            pl.when((mz <= t) & (mz > 0))(lambda: gather_left(c, t).wait_send())


def hand_over(a_in, b_in, a_out, b_out, sem):
    copies = [
        pltpu.make_async_copy(a_in, a_out, sem.at[0]),
        pltpu.make_async_copy(b_in, b_out, sem.at[1]),
    ]
    for copy in copies:
        copy.start()
    for copy in copies:
        copy.wait()


def lookup(table_values, index_rows, count_all):
    matched = index_rows[..., None] == jnp.arange(count_all, dtype=jnp.int32)
    return jnp.sum(jnp.where(matched, table_values, 0), axis=-1)


def on_device(
    hidden, group_qkv, mlp_branch, key_cache, paged_value_cache, cache_lengths, page_table,
    dense_weight, dense_bias, norm_gain, norm_bias, qkv_weight, qkv_bias,
):
    tok_dev, share = hidden.shape
    pages = lax.axis_size("page")
    shares = lax.axis_size("head")
    me = lax.axis_index("page")
    requests = cache_lengths.shape[0]
    slots = key_cache.shape[0]
    heads = group_qkv.shape[1] // (3 * HEAD_SIZE)
    width = heads * HEAD_SIZE
    every = tok_dev * pages
    vmem = pl.BlockSpec(memory_space=pltpu.VMEM)
    anywhere = pl.BlockSpec(memory_space=pl.ANY)
    dma = pltpu.SemaphoreType.DMA

    global_rows = me * tok_dev + jnp.arange(tok_dev, dtype=jnp.int32)
    positions = lookup(cache_lengths, global_rows // GROUP, requests) + global_rows % GROUP
    lane = jnp.arange(HEAD_SIZE, dtype=jnp.int32)
    half = ROT // 2
    inverse = 1.0 / 10000.0 ** ((2 * (lane % half)).astype(F32) / ROT)
    angles = positions.astype(F32)[:, None] * inverse[None, :]
    turned = lane[None, :] < ROT
    sine = jnp.sin(angles)
    table = jnp.stack(
        [
            jnp.where(turned, jnp.cos(angles), 1.0),
            jnp.where(turned, jnp.where(lane[None, :] < half, -sine, sine), 0.0),
        ]
    )

    q_all, kv_all = pl.pallas_call(
        functools.partial(gather_kernel, heads),
        out_shape=(
            jax.ShapeDtypeStruct((every, width), BF16),
            jax.ShapeDtypeStruct((every, 2 * width), BF16),
        ),
        in_specs=[vmem, vmem],
        out_specs=(anywhere, anywhere),
        scratch_shapes=[
            pltpu.VMEM((tok_dev, width), BF16),
            pltpu.VMEM((tok_dev, 2 * width), BF16),
            dma((3, max(4, pages // 2))),
            dma((3, max(4, pages // 2))),
            dma((3, max(5, pages // 2))),
            dma((3, max(5, pages // 2))),
            dma((2,)),
        ],
        compiler_params=pltpu.CompilerParams(
            collective_id=0, has_side_effects=True, vmem_limit_bytes=LIMIT
        ),
        name="gather_qkv",
    )(group_qkv, table)

    factor = math.log2(math.e) / math.sqrt(HEAD_SIZE)
    smem = pl.BlockSpec(memory_space=pltpu.SMEM)
    key_out, value_out, partial, stats = pl.pallas_call(
        functools.partial(attention_kernel, heads, factor),
        out_shape=(
            jax.ShapeDtypeStruct(key_cache.shape, BF16),
            jax.ShapeDtypeStruct(key_cache.shape, BF16),
            jax.ShapeDtypeStruct((pages, width, tok_dev), BF16),
            jax.ShapeDtypeStruct((pages, 16, tok_dev), F32),
        ),
        in_specs=[smem, smem, anywhere, anywhere, anywhere, anywhere],
        out_specs=(anywhere, anywhere, vmem, vmem),
        scratch_shapes=[
            pltpu.VMEM((every, width), BF16),
            pltpu.VMEM((every, 2 * width), BF16),
            pltpu.VMEM(key_cache.shape, BF16),
            pltpu.VMEM(key_cache.shape, BF16),
            pltpu.VMEM((requests, width, GROUP), F32),
            pltpu.VMEM((requests, 8, GROUP), F32),
            pltpu.VMEM((requests, 8, GROUP), F32),
            pltpu.SMEM((slots + 1,), jnp.int32),
            dma((2, slots)),
            dma((2, slots)),
            dma((2,)),
        ],
        compiler_params=pltpu.CompilerParams(vmem_limit_bytes=LIMIT),
        name="attend_slots",
    )(cache_lengths, page_table, q_all, kv_all, key_cache, paged_value_cache)

    chips = pages // 2
    chunks = 4
    stream_share, projected = pl.pallas_call(
        functools.partial(tail_kernel, heads, chunks),
        out_shape=(
            jax.ShapeDtypeStruct(hidden.shape, BF16),
            jax.ShapeDtypeStruct(group_qkv.shape, BF16),
        ),
        in_specs=[vmem, vmem, vmem, vmem, anywhere, vmem, vmem, vmem, anywhere, vmem],
        out_specs=(vmem, vmem),
        scratch_shapes=[
            *[
                pltpu.VMEM((chips,) + shape, kind)
                for _ in range(3)
                for shape, kind in (((width, tok_dev), BF16), ((16, tok_dev), F32))
            ],
            pltpu.VMEM(dense_weight.shape, BF16),
            pltpu.VMEM(qkv_weight.shape, BF16),
            pltpu.VMEM((tok_dev, width), BF16),
            *[pltpu.VMEM((shares, tok_dev, share), BF16) for _ in range(6)],
            pltpu.VMEM((tok_dev, share * shares), BF16),
            pltpu.VMEM((tok_dev, share), F32),
            dma((2,)),
            *[dma((2, chips)) for _ in range(4)],
            *[dma((chunks, shares)) for _ in range(8)],
        ],
        compiler_params=pltpu.CompilerParams(
            collective_id=1, has_side_effects=True, vmem_limit_bytes=LIMIT
        ),
        name="combine_project",
    )(
        partial, stats, hidden, mlp_branch, dense_weight, dense_bias[None, :], norm_gain[None, :],
        norm_bias[None, :], qkv_weight, qkv_bias[None, :],
    )
    new_hidden, next_qkv = pl.pallas_call(
        hand_over,
        out_shape=(
            jax.ShapeDtypeStruct(hidden.shape, BF16),
            jax.ShapeDtypeStruct(group_qkv.shape, BF16),
        ),
        in_specs=[anywhere, anywhere],
        out_specs=(anywhere, anywhere),
        scratch_shapes=[dma((2,))],
        name="hand_over",
    )(stream_share, projected)
    return new_hidden, next_qkv, key_out, value_out


def solution(mesh):
    in_specs = (
        P("page", "head"), P("page", "head"), P("page", "head"),
        P("page", None, "head"), P("page", None, "head"),
        P(), P(), P("head", None), P(), P(), P(), P(None, "head"), P("head"),
    )
    out_specs = (
        P("page", "head"), P("page", "head"), P("page", None, "head"), P("page", None, "head"),
    )
    return jax.shard_map(
        on_device, mesh=mesh, in_specs=in_specs, out_specs=out_specs, check_vma=False
    )
```

```python
import functools
import math

import jax
import jax.numpy as jnp
from jax import lax
from jax.experimental import pallas as pl
from jax.experimental.pallas import tpu as pltpu
from jax.sharding import PartitionSpec as P

HEAD_SIZE = 128
ROT = 32
PAGE_TOKENS = 128
GROUP = 512
MESH = pl.DeviceIdType.MESH
FLOOR = -1e29
MASKED = -1e30
LIMIT = 56 * 1024 * 1024
BF16 = jnp.bfloat16
F32 = jnp.float32


def signal_all(axes):
    barrier = pltpu.get_barrier_semaphore()
    count = 0
    for axis in axes:
        size = lax.axis_size(axis)
        me = lax.axis_index(axis)
        for offset in range(1, size):
            pl.semaphore_signal(
                barrier,
                inc=1,
                device_id={axis: lax.rem(me + offset, size)},
                device_id_type=MESH,
            )
            count += 1
    return barrier, count


def gather_kernel(heads, x_ref, table_ref, q_ref, kv_ref, q_mine, kv_mine, send, recv, fsend, frecv, lsem):
    pages = lax.axis_size("page")
    chips = pages // 2
    me = lax.axis_index("page")
    chip = lax.div(me, 2)
    core = lax.rem(me, 2)
    sibling = chip * 2 + 1 - core
    rows = x_ref.shape[0]
    width = heads * HEAD_SIZE
    lane = lax.broadcasted_iota(jnp.int32, (rows, HEAD_SIZE), 1)
    barrier, count = signal_all(("page",))

    def rotated(column):
        x = x_ref[:, column : column + HEAD_SIZE].astype(F32)
        ahead = pltpu.roll(x, HEAD_SIZE - ROT // 2, 1)
        behind = pltpu.roll(x, ROT // 2, 1)
        other = jnp.where(lane < ROT // 2, ahead, behind)
        return (x * table_ref[0] + other * table_ref[1]).astype(BF16)

    for head in range(heads):
        base = head * 3 * HEAD_SIZE
        at = head * HEAD_SIZE
        q_mine[:, at : at + HEAD_SIZE] = rotated(base)
        kv_mine[:, at : at + HEAD_SIZE] = rotated(base + HEAD_SIZE)
        kv_mine[:, width + at : width + at + HEAD_SIZE] = x_ref[
            :, base + 2 * HEAD_SIZE : base + 3 * HEAD_SIZE
        ]

    pieces = (
        (q_mine, q_ref, slice(0, width)),
        (kv_mine, kv_ref, slice(0, width)),
        (kv_mine, kv_ref, slice(width, 2 * width)),
    )

    def source_of(piece):
        src, _, columns = pieces[piece]
        return src.at[:, columns]

    def block_of(piece, index, begin=0, size=rows):
        _, dst, columns = pieces[piece]
        return dst.at[pl.ds(pl.multiple_of(index * rows + begin, 16), size), columns]

    def push(src, dst, target, send_sem, recv_sem):
        copy = pltpu.make_async_remote_copy(
            src_ref=src,
            dst_ref=dst,
            send_sem=send_sem,
            recv_sem=recv_sem,
            device_id={"page": target},
            device_id_type=MESH,
        )
        copy.start()
        return copy

    local = []
    for which, (src, dst) in enumerate(((q_mine, q_ref), (kv_mine, kv_ref))):
        copy = pltpu.make_async_copy(
            src, dst.at[pl.ds(pl.multiple_of(me * rows, rows), rows), :], lsem.at[which]
        )
        copy.start()
        local.append(copy)
    pl.semaphore_wait(barrier, count)

    first, forwards = [], []

    def forward(piece, index, kind, begin=0, size=rows):
        landed = block_of(piece, index, begin, size)
        forwards.append(push(landed, landed, sibling, fsend.at[piece, kind], frecv.at[piece, kind]))

    span = range(len(pieces))
    if chips == 4:
        x = lax.rem(chip, 2)
        across = (chip + 1 - 2 * x) * 2 + core
        along = lax.rem(chip + 2, 4) * 2 + core
        corner = lax.rem(chip + 3 - 2 * x, 4) * 2 + core
        half = rows // 2
        from_across, from_along = [], []
        for piece in span:
            src, dst = source_of(piece), block_of(piece, me)
            from_across.append(push(src, dst, across, send.at[piece, 0], recv.at[piece, 0]))
            from_along.append(push(src, dst, along, send.at[piece, 1], recv.at[piece, 1]))
            forwards.append(push(src, dst, sibling, fsend.at[piece, 0], frecv.at[piece, 0]))
        low, high = [], []
        for piece in span:
            from_across[piece].wait_recv()
            landed = block_of(piece, across, 0, half)
            low.append(push(landed, landed, along, send.at[piece, 2], recv.at[piece, 2]))
            from_along[piece].wait_recv()
            landed = block_of(piece, along, half, half)
            high.append(push(landed, landed, across, send.at[piece, 3], recv.at[piece, 3]))
            forward(piece, across, 1)
            forward(piece, along, 2)
        for piece in span:
            low[piece].wait_recv()
            forward(piece, corner, 3, 0, half)
            high[piece].wait_recv()
            forward(piece, corner, 4, half, half)
        first = from_across + from_along + low + high
    else:
        for piece in span:
            src, dst = source_of(piece), block_of(piece, me)
            for offset in range(1, chips):
                target = lax.rem(chip + offset, chips) * 2 + core
                first.append(push(src, dst, target, send.at[piece, offset], recv.at[piece, offset]))
            forwards.append(push(src, dst, sibling, fsend.at[piece, 0], frecv.at[piece, 0]))
        for piece in span:
            for offset in range(1, chips):
                first[piece * (chips - 1) + offset - 1].wait_recv()
                forward(piece, lax.rem(chip + chips - offset, chips) * 2 + core, offset)
    for copy in local:
        copy.wait()
    for copy in first:
        copy.wait_send()
    for copy in forwards:
        copy.wait()


def attention_kernel(
    heads, factor,
    len_ref, table_ref, q_hbm, kv_hbm, kc_hbm, vc_hbm,
    ko_hbm, vo_hbm, o_ref, st_ref,
    q_ref, kv_ref, keys, values, acc, m_s, l_s, code, in_sem, out_sem, q_sem,
):
    requests, max_pages = table_ref.shape
    slots = keys.shape[0]
    width = heads * HEAD_SIZE
    tok_dev = o_ref.shape[2]
    base = lax.axis_index("page") * slots

    load_q = pltpu.make_async_copy(q_hbm, q_ref, q_sem.at[0])
    load_kv = pltpu.make_async_copy(kv_hbm, kv_ref, q_sem.at[1])
    load_q.start()

    def page_in(slot):
        return (
            pltpu.make_async_copy(kc_hbm.at[slot], keys.at[slot], in_sem.at[0, slot]),
            pltpu.make_async_copy(vc_hbm.at[slot], values.at[slot], in_sem.at[1, slot]),
        )

    def page_out(slot):
        return (
            pltpu.make_async_copy(keys.at[slot], ko_hbm.at[slot], out_sem.at[0, slot]),
            pltpu.make_async_copy(values.at[slot], vo_hbm.at[slot], out_sem.at[1, slot]),
        )

    for slot in range(slots):
        for copy in page_in(slot):
            copy.start()
        if slot == 0:
            load_kv.start()
    for slot in range(slots + 1):
        code[slot] = 0
    for r in range(requests):

        def place(i, _):
            slot = table_ref[r, i] - base
            held = (slot >= 0) & (slot < slots)
            code[jnp.where(held, slot, slots)] = r * max_pages + i + 1
            return 0

        lax.fori_loop(0, max_pages, place, 0)
    acc[...] = jnp.zeros_like(acc)
    m_s[...] = jnp.full_like(m_s, FLOOR)
    l_s[...] = jnp.zeros_like(l_s)
    load_q.wait()
    load_kv.wait()

    def attend(slot, request, start, masked):
        mine = pl.ds(pl.multiple_of(request * GROUP, GROUP), GROUP)
        for head in range(heads):
            at = slice(head * HEAD_SIZE, (head + 1) * HEAD_SIZE)
            scores = (
                lax.dot_general(
                    keys[slot, :, at], q_ref[mine, at], (((1,), (1,)), ((), ())),
                    preferred_element_type=F32,
                )
                * factor
            )
            if masked:
                row = start + lax.broadcasted_iota(jnp.int32, scores.shape, 0)
                column = lax.broadcasted_iota(jnp.int32, scores.shape, 1)
                scores = jnp.where(row <= column, scores, MASKED)
            m_old = m_s[request, head : head + 1, :]
            m_new = jnp.maximum(m_old, jnp.max(scores, axis=0, keepdims=True))
            fade = jnp.exp2(m_old - m_new)
            weights = jnp.exp2(scores - m_new)
            m_s[request, head : head + 1, :] = m_new
            l_s[request, head : head + 1, :] = l_s[request, head : head + 1, :] * fade + jnp.sum(
                weights, axis=0, keepdims=True
            )
            part = lax.dot_general(
                values[slot, :, at], weights.astype(BF16), (((0,), (0,)), ((), ())),
                preferred_element_type=F32,
            )
            acc[request, at, :] = acc[request, at, :] * fade + part

    def step(slot, _):
        for copy in page_in(slot):
            copy.wait()
        known = code[slot]
        entry = jnp.maximum(known - 1, 0)
        request = lax.div(entry, max_pages)
        start = lax.rem(entry, max_pages) * PAGE_TOKENS - len_ref[request]
        live = (known > 0) & (start < GROUP)
        old = live & (start <= -PAGE_TOKENS)
        new = live & (start > -PAGE_TOKENS)

        @pl.when(new)
        def _():
            mine = pl.ds(pl.multiple_of(request * GROUP, GROUP), GROUP)
            row = start + lax.broadcasted_iota(jnp.int32, (PAGE_TOKENS, GROUP), 0)
            column = lax.broadcasted_iota(jnp.int32, (PAGE_TOKENS, GROUP), 1)
            pick = jnp.where(row == column, 1.0, 0.0).astype(BF16)
            place = start + lax.broadcasted_iota(jnp.int32, (PAGE_TOKENS, width), 0)
            fresh = (place >= 0) & (place < GROUP)
            for part, held in enumerate((keys, values)):
                moved = jnp.dot(
                    pick, kv_ref[mine, part * width : (part + 1) * width], preferred_element_type=F32
                )
                held[slot] = jnp.where(fresh, moved, held[slot].astype(F32)).astype(BF16)

        for copy in page_out(slot):
            copy.start()
        pl.when(old)(lambda: attend(slot, request, start, False))
        pl.when(new)(lambda: attend(slot, request, start, True))
        return 0

    lax.fori_loop(0, slots, step, 0)

    per = GROUP // tok_dev
    for r in range(requests):
        for b in range(per):
            columns = slice(b * tok_dev, (b + 1) * tok_dev)
            o_ref[r * per + b] = acc[r, :, columns].astype(BF16)
            st_ref[r * per + b, 0:8, :] = m_s[r, :, columns]
            st_ref[r * per + b, 8:16, :] = l_s[r, :, columns]

    def drain(slot, _):
        for copy in page_out(slot):
            copy.wait()
        return 0

    lax.fori_loop(0, slots, drain, 0)


def tail_kernel(
    heads, chunks,
    o_ref, st_ref, hidden_ref, branch_ref, dw_ref, dbias_ref, gain_ref, nbias_ref, qw_ref, qbias_ref,
    hid_out, qkv_out,
    o_sib, st_sib, o_pair, st_pair, o_in, st_in, dw, qw, att, proj,
    near_in, far_in, relay_in, relay_out, stream, normed, total,
    wsem, bsend, brecv, osend, orecv,
    nsend, nrecv, fsend, frecv, rsend, rrecv, gsend, grecv, hsend, hrecv, tsend, trecv,
):
    pages = lax.axis_size("page")
    chips = pages // 2
    shares = lax.axis_size("head")
    me = lax.axis_index("page")
    mz = lax.axis_index("head")
    chip = lax.div(me, 2)
    core = lax.rem(me, 2)
    rows, share = hidden_ref.shape
    model = share * shares
    piece = rows // chunks

    load_dw = pltpu.make_async_copy(dw_ref, dw, wsem.at[0])
    load_qw = pltpu.make_async_copy(qw_ref, qw, wsem.at[1])
    load_dw.start()
    barrier, count = signal_all(("page", "head"))
    pl.semaphore_wait(barrier, count)

    def page_push(src, dst, target, send_sem, recv_sem):
        copy = pltpu.make_async_remote_copy(
            src_ref=src,
            dst_ref=dst,
            send_sem=send_sem,
            recv_sem=recv_sem,
            device_id={"page": target},
            device_id_type=MESH,
        )
        copy.start()
        return copy

    order = list(range(chips - 1, 0, -1)) + [0]
    shared = {}
    for k in order:
        theirs = lax.rem(chip + k, chips) * 2 + 1 - core
        shared[k] = (
            page_push(st_ref.at[theirs], st_sib.at[k], chip * 2 + 1 - core, bsend.at[0, k], brecv.at[0, k]),
            page_push(o_ref.at[theirs], o_sib.at[k], chip * 2 + 1 - core, bsend.at[1, k], brecv.at[1, k]),
        )
    load_qw.start()
    sent = []
    for k in order:
        for copy in shared[k]:
            copy.wait()
        ours = lax.rem(chip + k, chips) * 2 + core
        for head in range(heads):
            at = slice(head * HEAD_SIZE, (head + 1) * HEAD_SIZE)
            m_mine = st_ref[ours, head : head + 1, :]
            m_sib = st_sib[k, head : head + 1, :]
            peak = jnp.maximum(m_mine, m_sib)
            e_mine = jnp.exp2(m_mine - peak)
            e_sib = jnp.exp2(m_sib - peak)
            st_pair[k, head : head + 1, :] = peak
            st_pair[k, 8 + head : 9 + head, :] = (
                st_ref[ours, 8 + head : 9 + head, :] * e_mine + st_sib[k, 8 + head : 9 + head, :] * e_sib
            )
            o_pair[k, at, :] = (
                o_ref[ours, at, :].astype(F32) * e_mine + o_sib[k, at, :].astype(F32) * e_sib
            ).astype(BF16)
        if k:
            sent.append(page_push(st_pair.at[k], st_in.at[k], ours, osend.at[0, k], orecv.at[0, k]))
            sent.append(page_push(o_pair.at[k], o_in.at[k], ours, osend.at[1, k], orecv.at[1, k]))
    st_in[0] = st_pair[0]
    o_in[0] = o_pair[0]
    total[...] = dbias_ref[:, pl.ds(pl.multiple_of(mz * share, share), share)] + (
        hidden_ref[...].astype(F32) + branch_ref[...].astype(F32)
    )
    for copy in sent:
        copy.wait()

    for head in range(heads):
        at = slice(head * HEAD_SIZE, (head + 1) * HEAD_SIZE)

        def raise_peak(j, peak):
            return jnp.maximum(peak, st_in[j, head : head + 1, :])

        peak = lax.fori_loop(1, chips, raise_peak, st_in[0, head : head + 1, :])

        def add(j, pair):
            summed, count = pair
            scale = jnp.exp2(st_in[j, head : head + 1, :] - peak)
            return (
                summed + o_in[j, at, :].astype(F32) * scale,
                count + st_in[j, 8 + head : 9 + head, :] * scale,
            )

        summed, count = lax.fori_loop(
            0, chips, add, (jnp.zeros((HEAD_SIZE, rows), F32), jnp.zeros((1, rows), F32))
        )
        att[:, at] = (summed / count).T.astype(BF16)
    load_dw.wait()
    outer = (mz == 0) | (mz == shares - 1)
    inner = jnp.logical_not(outer)
    partner = mz + 1 - 2 * lax.rem(mz, 2)
    far_inner = jnp.where(mz < 2, 2, 1)
    far_outer = jnp.where(mz < 2, 3, 0)
    far = (far_outer, far_inner)
    rank = jnp.where(outer, 0, 1)

    def project(t):
        columns = pl.ds(pl.multiple_of(t * share, share), share)
        return jnp.dot(att[...], dw[:, columns], preferred_element_type=F32)

    for k, t in enumerate((*far, partner)):
        proj[k] = project(t).astype(BF16)

    def z_copy(src, dst, send_sem, recv_sem, target, c):
        at = pl.ds(c * piece, piece)
        return pltpu.make_async_remote_copy(
            src_ref=src.at[at, :],
            dst_ref=dst.at[at, :],
            send_sem=send_sem,
            recv_sem=recv_sem,
            device_id={"head": target},
            device_id_type=MESH,
        )

    def term_near(c):
        return z_copy(proj.at[2], near_in, nsend.at[c], nrecv.at[c], partner, c)

    def term_up(c, k):
        return z_copy(proj.at[k], relay_in.at[k], rsend.at[c, k], rrecv.at[c, k], partner, c)

    def term_far(c, k):
        return z_copy(relay_out.at[k], far_in, fsend.at[c, k], frecv.at[c], far[k], c)

    def block_near(c):
        return z_copy(stream.at[mz], stream.at[mz], gsend.at[c], grecv.at[c], partner, c)

    def block_far(c):
        return z_copy(stream.at[mz], stream.at[mz], hsend.at[c], hrecv.at[c, rank], far_inner, c)

    def block_down(c, k):
        return z_copy(stream.at[far[k]], stream.at[far[k]], tsend.at[c, k], trecv.at[c, k], partner, c)

    def rows_of(c):
        return slice(c * piece, (c + 1) * piece)

    for c in range(chunks):

        @pl.when(outer)
        def _():
            for k in range(2):
                term_up(c, k).start()

        term_near(c).start()
    total[...] += project(mz)

    for c in range(chunks):
        at = rows_of(c)

        @pl.when(inner)
        def _():
            for k in range(2):
                term_up(c, k).wait_recv()
                relay_out[k, at, :] = (
                    proj[k, at, :].astype(F32) + relay_in[k, at, :].astype(F32)
                ).astype(BF16)
                term_far(c, k).start()

    for c in range(chunks):
        at = rows_of(c)
        term_near(c).wait_recv()
        term_far(c, 0).wait_recv()
        mine = (total[at, :] + near_in[at, :].astype(F32) + far_in[at, :].astype(F32)).astype(BF16)
        hid_out[at, :] = mine
        stream[mz, at, :] = mine
        block_far(c).start()
        block_near(c).start()

    def norm_chunk(c):
        at = rows_of(c)
        first = jnp.zeros((piece, 1), F32)
        second = jnp.zeros((piece, 1), F32)
        for j in range(shares):
            x = stream[j, at, :].astype(F32)
            first += jnp.sum(x, axis=1, keepdims=True)
            second += jnp.sum(x * x, axis=1, keepdims=True)
        mean = first / model
        scale = lax.rsqrt(second / model - mean * mean + 1e-05)
        for j in range(shares):
            columns = slice(j * share, (j + 1) * share)
            x = stream[j, at, :].astype(F32)
            normed[at, columns] = (
                (x - mean) * scale * gain_ref[:, columns] + nbias_ref[:, columns]
            ).astype(BF16)
        block = 256
        for j in range(qkv_out.shape[1] // block):
            columns = slice(j * block, (j + 1) * block)
            out = jnp.dot(normed[at, :], qw[:, columns], preferred_element_type=F32)
            qkv_out[at, columns] = (out + qbias_ref[:, columns]).astype(BF16)

    load_qw.wait()
    for c in range(chunks):

        @pl.when(inner)
        def _():
            for k in (1, 0):
                z_copy(
                    stream.at[far[k]], stream.at[far[k]], hsend.at[c], hrecv.at[c, k], far_inner, c
                ).wait_recv()
                block_down(c, k).start()

    for c in range(chunks):
        block_near(c).wait_recv()

        @pl.when(outer)
        def _():
            for k in range(2):
                block_down(c, k).wait_recv()

        norm_chunk(c)

    for c in range(chunks):
        term_near(c).wait_send()
        block_near(c).wait_send()
        block_far(c).wait_send()
        for k in range(2):
            pl.when(outer)(lambda: term_up(c, k).wait_send())
            pl.when(inner)(lambda: term_far(c, k).wait_send())
            pl.when(inner)(lambda: block_down(c, k).wait_send())


def hand_over(a_in, b_in, a_out, b_out):
    a_out[...] = a_in[...]
    b_out[...] = b_in[...]


def lookup(table_values, index_rows, count_all):
    matched = index_rows[..., None] == jnp.arange(count_all, dtype=jnp.int32)
    return jnp.sum(jnp.where(matched, table_values, 0), axis=-1)


def on_device(
    hidden, group_qkv, mlp_branch, key_cache, paged_value_cache, cache_lengths, page_table,
    dense_weight, dense_bias, norm_gain, norm_bias, qkv_weight, qkv_bias,
):
    tok_dev, share = hidden.shape
    pages = lax.axis_size("page")
    shares = lax.axis_size("head")
    me = lax.axis_index("page")
    requests = cache_lengths.shape[0]
    slots = key_cache.shape[0]
    heads = group_qkv.shape[1] // (3 * HEAD_SIZE)
    width = heads * HEAD_SIZE
    every = tok_dev * pages
    vmem = pl.BlockSpec(memory_space=pltpu.VMEM)
    anywhere = pl.BlockSpec(memory_space=pl.ANY)
    dma = pltpu.SemaphoreType.DMA

    global_rows = me * tok_dev + jnp.arange(tok_dev, dtype=jnp.int32)
    positions = lookup(cache_lengths, global_rows // GROUP, requests) + global_rows % GROUP
    lane = jnp.arange(HEAD_SIZE, dtype=jnp.int32)
    half = ROT // 2
    inverse = 1.0 / 10000.0 ** ((2 * (lane % half)).astype(F32) / ROT)
    angles = positions.astype(F32)[:, None] * inverse[None, :]
    turned = lane[None, :] < ROT
    sine = jnp.sin(angles)
    table = jnp.stack(
        [
            jnp.where(turned, jnp.cos(angles), 1.0),
            jnp.where(turned, jnp.where(lane[None, :] < half, -sine, sine), 0.0),
        ]
    )

    q_all, kv_all = pl.pallas_call(
        functools.partial(gather_kernel, heads),
        out_shape=(
            jax.ShapeDtypeStruct((every, width), BF16),
            jax.ShapeDtypeStruct((every, 2 * width), BF16),
        ),
        in_specs=[vmem, vmem],
        out_specs=(anywhere, anywhere),
        scratch_shapes=[
            pltpu.VMEM((tok_dev, width), BF16),
            pltpu.VMEM((tok_dev, 2 * width), BF16),
            dma((3, max(4, pages // 2))),
            dma((3, max(4, pages // 2))),
            dma((3, max(5, pages // 2))),
            dma((3, max(5, pages // 2))),
            dma((2,)),
        ],
        compiler_params=pltpu.CompilerParams(
            collective_id=0, has_side_effects=True, vmem_limit_bytes=LIMIT
        ),
        name="gather_qkv",
    )(group_qkv, table)

    factor = math.log2(math.e) / math.sqrt(HEAD_SIZE)
    smem = pl.BlockSpec(memory_space=pltpu.SMEM)
    key_out, value_out, partial, stats = pl.pallas_call(
        functools.partial(attention_kernel, heads, factor),
        out_shape=(
            jax.ShapeDtypeStruct(key_cache.shape, BF16),
            jax.ShapeDtypeStruct(key_cache.shape, BF16),
            jax.ShapeDtypeStruct((pages, width, tok_dev), BF16),
            jax.ShapeDtypeStruct((pages, 16, tok_dev), F32),
        ),
        in_specs=[smem, smem, anywhere, anywhere, anywhere, anywhere],
        out_specs=(anywhere, anywhere, vmem, vmem),
        scratch_shapes=[
            pltpu.VMEM((every, width), BF16),
            pltpu.VMEM((every, 2 * width), BF16),
            pltpu.VMEM(key_cache.shape, BF16),
            pltpu.VMEM(key_cache.shape, BF16),
            pltpu.VMEM((requests, width, GROUP), F32),
            pltpu.VMEM((requests, 8, GROUP), F32),
            pltpu.VMEM((requests, 8, GROUP), F32),
            pltpu.SMEM((slots + 1,), jnp.int32),
            dma((2, slots)),
            dma((2, slots)),
            dma((2,)),
        ],
        compiler_params=pltpu.CompilerParams(vmem_limit_bytes=LIMIT),
        name="attend_slots",
    )(cache_lengths, page_table, q_all, kv_all, key_cache, paged_value_cache)

    chips = pages // 2
    chunks = 2
    stream_share, projected = pl.pallas_call(
        functools.partial(tail_kernel, heads, chunks),
        out_shape=(
            jax.ShapeDtypeStruct(hidden.shape, BF16),
            jax.ShapeDtypeStruct(group_qkv.shape, BF16),
        ),
        in_specs=[vmem, vmem, vmem, vmem, anywhere, vmem, vmem, vmem, anywhere, vmem],
        out_specs=(vmem, vmem),
        scratch_shapes=[
            *[
                pltpu.VMEM((chips,) + shape, kind)
                for _ in range(3)
                for shape, kind in (((width, tok_dev), BF16), ((16, tok_dev), F32))
            ],
            pltpu.VMEM(dense_weight.shape, BF16),
            pltpu.VMEM(qkv_weight.shape, BF16),
            pltpu.VMEM((tok_dev, width), BF16),
            pltpu.VMEM((3, tok_dev, share), BF16),
            pltpu.VMEM((tok_dev, share), BF16),
            pltpu.VMEM((tok_dev, share), BF16),
            pltpu.VMEM((2, tok_dev, share), BF16),
            pltpu.VMEM((2, tok_dev, share), BF16),
            pltpu.VMEM((shares, tok_dev, share), BF16),
            pltpu.VMEM((tok_dev, share * shares), BF16),
            pltpu.VMEM((tok_dev, share), F32),
            dma((2,)),
            *[dma((2, chips)) for _ in range(4)],
            dma((chunks,)),
            dma((chunks,)),
            dma((chunks, 2)),
            dma((chunks,)),
            dma((chunks, 2)),
            dma((chunks, 2)),
            dma((chunks,)),
            dma((chunks,)),
            dma((chunks,)),
            dma((chunks, 2)),
            dma((chunks, 2)),
            dma((chunks, 2)),
        ],
        compiler_params=pltpu.CompilerParams(
            collective_id=1, has_side_effects=True, vmem_limit_bytes=LIMIT
        ),
        name="combine_project",
    )(
        partial, stats, hidden, mlp_branch, dense_weight, dense_bias[None, :], norm_gain[None, :],
        norm_bias[None, :], qkv_weight, qkv_bias[None, :],
    )
    new_hidden, next_qkv = pl.pallas_call(
        hand_over,
        out_shape=(
            jax.ShapeDtypeStruct(hidden.shape, BF16),
            jax.ShapeDtypeStruct(group_qkv.shape, BF16),
        ),
        in_specs=[vmem, vmem],
        out_specs=(vmem, vmem),
        name="hand_over",
    )(stream_share, projected)
    return new_hidden, next_qkv, key_out, value_out


def solution(mesh):
    in_specs = (
        P("page", "head"), P("page", "head"), P("page", "head"),
        P("page", None, "head"), P("page", None, "head"),
        P(), P(), P("head", None), P(), P(), P(), P(None, "head"), P("head"),
    )
    out_specs = (
        P("page", "head"), P("page", "head"), P("page", None, "head"), P("page", None, "head"),
    )
    return jax.shard_map(
        on_device, mesh=mesh, in_specs=in_specs, out_specs=out_specs, check_vma=False
    )
```

```python
import functools
import math

import jax
import jax.numpy as jnp
from jax import lax
from jax.experimental import pallas as pl
from jax.experimental.pallas import tpu as pltpu
from jax.sharding import PartitionSpec as P

HEAD_SIZE = 128
ROT = 32
PAGE_TOKENS = 128
GROUP = 512
MESH = pl.DeviceIdType.MESH
FLOOR = -1e29
MASKED = -1e30
LIMIT = 56 * 1024 * 1024
BF16 = jnp.bfloat16
F32 = jnp.float32


def signal_all(axes):
    barrier = pltpu.get_barrier_semaphore()
    count = 0
    for axis in axes:
        size = lax.axis_size(axis)
        me = lax.axis_index(axis)
        for offset in range(1, size):
            pl.semaphore_signal(
                barrier,
                inc=1,
                device_id={axis: lax.rem(me + offset, size)},
                device_id_type=MESH,
            )
            count += 1
    return barrier, count


def gather_kernel(heads, x_ref, table_ref, q_ref, kv_ref, q_mine, kv_mine, send, recv, fsend, frecv, lsem):
    pages = lax.axis_size("page")
    chips = pages // 2
    me = lax.axis_index("page")
    chip = lax.div(me, 2)
    core = lax.rem(me, 2)
    sibling = chip * 2 + 1 - core
    rows = x_ref.shape[0]
    width = heads * HEAD_SIZE
    lane = lax.broadcasted_iota(jnp.int32, (rows, HEAD_SIZE), 1)
    barrier, count = signal_all(("page",))

    def rotated(column):
        x = x_ref[:, column : column + HEAD_SIZE].astype(F32)
        ahead = pltpu.roll(x, HEAD_SIZE - ROT // 2, 1)
        behind = pltpu.roll(x, ROT // 2, 1)
        other = jnp.where(lane < ROT // 2, ahead, behind)
        return (x * table_ref[0] + other * table_ref[1]).astype(BF16)

    for head in range(heads):
        base = head * 3 * HEAD_SIZE
        at = head * HEAD_SIZE
        q_mine[:, at : at + HEAD_SIZE] = rotated(base)
        kv_mine[:, at : at + HEAD_SIZE] = rotated(base + HEAD_SIZE)
        kv_mine[:, width + at : width + at + HEAD_SIZE] = x_ref[
            :, base + 2 * HEAD_SIZE : base + 3 * HEAD_SIZE
        ]

    pieces = (
        (q_mine, q_ref, slice(0, width)),
        (kv_mine, kv_ref, slice(0, width)),
        (kv_mine, kv_ref, slice(width, 2 * width)),
    )

    def source_of(piece):
        src, _, columns = pieces[piece]
        return src.at[:, columns]

    def block_of(piece, index, begin=0, size=rows):
        _, dst, columns = pieces[piece]
        return dst.at[pl.ds(pl.multiple_of(index * rows + begin, 16), size), columns]

    def push(src, dst, target, send_sem, recv_sem):
        copy = pltpu.make_async_remote_copy(
            src_ref=src,
            dst_ref=dst,
            send_sem=send_sem,
            recv_sem=recv_sem,
            device_id={"page": target},
            device_id_type=MESH,
        )
        copy.start()
        return copy

    local = []
    for which, (src, dst) in enumerate(((q_mine, q_ref), (kv_mine, kv_ref))):
        copy = pltpu.make_async_copy(
            src, dst.at[pl.ds(pl.multiple_of(me * rows, rows), rows), :], lsem.at[which]
        )
        copy.start()
        local.append(copy)
    pl.semaphore_wait(barrier, count)

    first, forwards = [], []

    def forward(piece, index, kind, begin=0, size=rows):
        landed = block_of(piece, index, begin, size)
        forwards.append(push(landed, landed, sibling, fsend.at[piece, kind], frecv.at[piece, kind]))

    span = range(len(pieces))
    if chips == 4:
        x = lax.rem(chip, 2)
        across = (chip + 1 - 2 * x) * 2 + core
        along = lax.rem(chip + 2, 4) * 2 + core
        corner = lax.rem(chip + 3 - 2 * x, 4) * 2 + core
        half = rows // 2
        from_across, from_along = [], []
        for piece in span:
            src, dst = source_of(piece), block_of(piece, me)
            from_across.append(push(src, dst, across, send.at[piece, 0], recv.at[piece, 0]))
            from_along.append(push(src, dst, along, send.at[piece, 1], recv.at[piece, 1]))
            forwards.append(push(src, dst, sibling, fsend.at[piece, 0], frecv.at[piece, 0]))
        low, high = [], []
        for piece in span:
            from_across[piece].wait_recv()
            landed = block_of(piece, across, 0, half)
            low.append(push(landed, landed, along, send.at[piece, 2], recv.at[piece, 2]))
            from_along[piece].wait_recv()
            landed = block_of(piece, along, half, half)
            high.append(push(landed, landed, across, send.at[piece, 3], recv.at[piece, 3]))
            forward(piece, across, 1)
            forward(piece, along, 2)
        for piece in span:
            low[piece].wait_recv()
            forward(piece, corner, 3, 0, half)
            high[piece].wait_recv()
            forward(piece, corner, 4, half, half)
        first = from_across + from_along + low + high
    else:
        for piece in span:
            src, dst = source_of(piece), block_of(piece, me)
            for offset in range(1, chips):
                target = lax.rem(chip + offset, chips) * 2 + core
                first.append(push(src, dst, target, send.at[piece, offset], recv.at[piece, offset]))
            forwards.append(push(src, dst, sibling, fsend.at[piece, 0], frecv.at[piece, 0]))
        for piece in span:
            for offset in range(1, chips):
                first[piece * (chips - 1) + offset - 1].wait_recv()
                forward(piece, lax.rem(chip + chips - offset, chips) * 2 + core, offset)
    for copy in local:
        copy.wait()
    for copy in first:
        copy.wait_send()
    for copy in forwards:
        copy.wait()


def attention_kernel(
    heads, factor,
    len_ref, table_ref, q_hbm, kv_hbm, kc_hbm, vc_hbm,
    ko_hbm, vo_hbm, o_ref, st_ref,
    q_ref, kv_ref, keys, values, acc, m_s, l_s, code, in_sem, out_sem, q_sem,
):
    requests, max_pages = table_ref.shape
    slots = keys.shape[0]
    width = heads * HEAD_SIZE
    tok_dev = o_ref.shape[2]
    base = lax.axis_index("page") * slots

    load_q = pltpu.make_async_copy(q_hbm, q_ref, q_sem.at[0])
    load_kv = pltpu.make_async_copy(kv_hbm, kv_ref, q_sem.at[1])
    load_q.start()

    def page_in(slot):
        return (
            pltpu.make_async_copy(kc_hbm.at[slot], keys.at[slot], in_sem.at[0, slot]),
            pltpu.make_async_copy(vc_hbm.at[slot], values.at[slot], in_sem.at[1, slot]),
        )

    def page_out(slot):
        return (
            pltpu.make_async_copy(keys.at[slot], ko_hbm.at[slot], out_sem.at[0, slot]),
            pltpu.make_async_copy(values.at[slot], vo_hbm.at[slot], out_sem.at[1, slot]),
        )

    for slot in range(slots):
        for copy in page_in(slot):
            copy.start()
    load_kv.start()
    for slot in range(slots + 1):
        code[slot] = 0
    for r in range(requests):

        def place(i, _):
            slot = table_ref[r, i] - base
            held = (slot >= 0) & (slot < slots)
            code[jnp.where(held, slot, slots)] = r * max_pages + i + 1
            return 0

        lax.fori_loop(0, max_pages, place, 0)
    acc[...] = jnp.zeros_like(acc)
    m_s[...] = jnp.full_like(m_s, FLOOR)
    l_s[...] = jnp.zeros_like(l_s)
    load_q.wait()

    spans = [slice(head * HEAD_SIZE, (head + 1) * HEAD_SIZE) for head in range(heads)]

    def attend(slot, request, start, masked):
        mine = pl.ds(pl.multiple_of(request * GROUP, GROUP), GROUP)
        m_old = m_s[request, 0:heads, :]
        l_old = l_s[request, 0:heads, :]
        m_all, l_all, fades, parts = [], [], [], []
        for head, at in enumerate(spans):
            scores = (
                lax.dot_general(
                    keys[slot, :, at], q_ref[mine, at], (((1,), (1,)), ((), ())),
                    preferred_element_type=F32,
                )
                * factor
            )
            if masked:
                row = start + lax.broadcasted_iota(jnp.int32, scores.shape, 0)
                column = lax.broadcasted_iota(jnp.int32, scores.shape, 1)
                scores = jnp.where(row <= column, scores, MASKED)
            before = m_old[head : head + 1, :]
            m_new = jnp.maximum(before, jnp.max(scores, axis=0, keepdims=True))
            fade = jnp.exp2(before - m_new)
            weights = jnp.exp2(scores - m_new)
            m_all.append(m_new)
            l_all.append(l_old[head : head + 1, :] * fade + jnp.sum(weights, axis=0, keepdims=True))
            fades.append(fade)
            parts.append(
                lax.dot_general(
                    values[slot, :, at], weights.astype(BF16), (((0,), (0,)), ((), ())),
                    preferred_element_type=F32,
                )
            )
        for head, at in enumerate(spans):
            acc[request, at, :] = acc[request, at, :] * fades[head] + parts[head]
        m_s[request, 0:heads, :] = jnp.concatenate(m_all, axis=0)
        l_s[request, 0:heads, :] = jnp.concatenate(l_all, axis=0)

    def facts(slot):
        known = code[slot]
        entry = jnp.maximum(known - 1, 0)
        request = lax.div(entry, max_pages)
        start = lax.rem(entry, max_pages) * PAGE_TOKENS - len_ref[request]
        live = (known > 0) & (start < GROUP)
        return request, start, live & (start <= -PAGE_TOKENS), live & (start > -PAGE_TOKENS)

    def step(slot, _):
        for copy in page_in(slot):
            copy.wait()
        request, start, old, new = facts(slot)

        @pl.when(jnp.logical_not(new))
        def _():
            for copy in page_out(slot):
                copy.start()

        pl.when(old)(lambda: attend(slot, request, start, False))
        return 0

    lax.fori_loop(0, slots, step, 0)
    load_kv.wait()

    def fresh_step(slot, _):
        request, start, _, new = facts(slot)

        @pl.when(new)
        def _():
            mine = pl.ds(pl.multiple_of(request * GROUP, GROUP), GROUP)
            row = start + lax.broadcasted_iota(jnp.int32, (PAGE_TOKENS, GROUP), 0)
            column = lax.broadcasted_iota(jnp.int32, (PAGE_TOKENS, GROUP), 1)
            pick = jnp.where(row == column, 1.0, 0.0).astype(BF16)
            place = start + lax.broadcasted_iota(jnp.int32, (PAGE_TOKENS, width), 0)
            fresh = (place >= 0) & (place < GROUP)
            for part, held in enumerate((keys, values)):
                moved = jnp.dot(
                    pick, kv_ref[mine, part * width : (part + 1) * width], preferred_element_type=F32
                )
                held[slot] = jnp.where(fresh, moved, held[slot].astype(F32)).astype(BF16)
            for copy in page_out(slot):
                copy.start()
            attend(slot, request, start, True)

        return 0

    lax.fori_loop(0, slots, fresh_step, 0)

    per = GROUP // tok_dev
    for r in range(requests):
        for b in range(per):
            columns = slice(b * tok_dev, (b + 1) * tok_dev)
            o_ref[r * per + b] = acc[r, :, columns].astype(BF16)
            st_ref[r * per + b, 0:8, :] = m_s[r, :, columns]
            st_ref[r * per + b, 8:16, :] = l_s[r, :, columns]

    def drain(slot, _):
        for copy in page_out(slot):
            copy.wait()
        return 0

    lax.fori_loop(0, slots, drain, 0)


def tail_kernel(
    heads, chunks,
    o_ref, st_ref, hidden_ref, branch_ref, dw_ref, dbias_ref, gain_ref, nbias_ref, qw_ref, qbias_ref,
    hid_out, qkv_out,
    o_sib, st_sib, o_pair, st_pair, o_in, st_in, dw, qw, att, proj,
    near_in, far_in, relay_in, relay_out, stream, normed, total,
    wsem, bsend, brecv, osend, orecv,
    nsend, nrecv, fsend, frecv, rsend, rrecv, gsend, grecv, hsend, hrecv, tsend, trecv,
):
    pages = lax.axis_size("page")
    chips = pages // 2
    shares = lax.axis_size("head")
    me = lax.axis_index("page")
    mz = lax.axis_index("head")
    chip = lax.div(me, 2)
    core = lax.rem(me, 2)
    rows, share = hidden_ref.shape
    model = share * shares
    piece = rows // chunks

    load_dw = pltpu.make_async_copy(dw_ref, dw, wsem.at[0])
    load_qw = pltpu.make_async_copy(qw_ref, qw, wsem.at[1])
    load_dw.start()
    barrier, count = signal_all(("page", "head"))
    pl.semaphore_wait(barrier, count)

    def page_push(src, dst, target, send_sem, recv_sem):
        copy = pltpu.make_async_remote_copy(
            src_ref=src,
            dst_ref=dst,
            send_sem=send_sem,
            recv_sem=recv_sem,
            device_id={"page": target},
            device_id_type=MESH,
        )
        copy.start()
        return copy

    order = list(range(chips - 1, 0, -1)) + [0]
    shared = {}
    for k in order:
        theirs = lax.rem(chip + k, chips) * 2 + 1 - core
        shared[k] = (
            page_push(st_ref.at[theirs], st_sib.at[k], chip * 2 + 1 - core, bsend.at[0, k], brecv.at[0, k]),
            page_push(o_ref.at[theirs], o_sib.at[k], chip * 2 + 1 - core, bsend.at[1, k], brecv.at[1, k]),
        )
    load_qw.start()
    sent = []
    for k in order:
        for copy in shared[k]:
            copy.wait()
        ours = lax.rem(chip + k, chips) * 2 + core
        for head in range(heads):
            at = slice(head * HEAD_SIZE, (head + 1) * HEAD_SIZE)
            m_mine = st_ref[ours, head : head + 1, :]
            m_sib = st_sib[k, head : head + 1, :]
            peak = jnp.maximum(m_mine, m_sib)
            e_mine = jnp.exp2(m_mine - peak)
            e_sib = jnp.exp2(m_sib - peak)
            st_pair[k, head : head + 1, :] = peak
            st_pair[k, 8 + head : 9 + head, :] = (
                st_ref[ours, 8 + head : 9 + head, :] * e_mine + st_sib[k, 8 + head : 9 + head, :] * e_sib
            )
            o_pair[k, at, :] = (
                o_ref[ours, at, :].astype(F32) * e_mine + o_sib[k, at, :].astype(F32) * e_sib
            ).astype(BF16)
        if k:
            sent.append(page_push(st_pair.at[k], st_in.at[k], ours, osend.at[0, k], orecv.at[0, k]))
            sent.append(page_push(o_pair.at[k], o_in.at[k], ours, osend.at[1, k], orecv.at[1, k]))
    st_in[0] = st_pair[0]
    o_in[0] = o_pair[0]
    total[...] = dbias_ref[:, pl.ds(pl.multiple_of(mz * share, share), share)] + (
        hidden_ref[...].astype(F32) + branch_ref[...].astype(F32)
    )
    for copy in sent:
        copy.wait()

    for head in range(heads):
        at = slice(head * HEAD_SIZE, (head + 1) * HEAD_SIZE)

        def raise_peak(j, peak):
            return jnp.maximum(peak, st_in[j, head : head + 1, :])

        peak = lax.fori_loop(1, chips, raise_peak, st_in[0, head : head + 1, :])

        def add(j, pair):
            summed, count = pair
            scale = jnp.exp2(st_in[j, head : head + 1, :] - peak)
            return (
                summed + o_in[j, at, :].astype(F32) * scale,
                count + st_in[j, 8 + head : 9 + head, :] * scale,
            )

        summed, count = lax.fori_loop(
            0, chips, add, (jnp.zeros((HEAD_SIZE, rows), F32), jnp.zeros((1, rows), F32))
        )
        att[:, at] = (summed / count).T.astype(BF16)
    load_dw.wait()
    outer = (mz == 0) | (mz == shares - 1)
    inner = jnp.logical_not(outer)
    partner = mz + 1 - 2 * lax.rem(mz, 2)
    far_inner = jnp.where(mz < 2, 2, 1)
    far_outer = jnp.where(mz < 2, 3, 0)
    far = (far_outer, far_inner)
    rank = jnp.where(outer, 0, 1)

    def project(t):
        columns = pl.ds(pl.multiple_of(t * share, share), share)
        return jnp.dot(att[...], dw[:, columns], preferred_element_type=F32)

    for k, t in enumerate((*far, partner)):
        proj[k] = project(t).astype(BF16)

    def z_copy(src, dst, send_sem, recv_sem, target, c):
        at = pl.ds(c * piece, piece)
        return pltpu.make_async_remote_copy(
            src_ref=src.at[at, :],
            dst_ref=dst.at[at, :],
            send_sem=send_sem,
            recv_sem=recv_sem,
            device_id={"head": target},
            device_id_type=MESH,
        )

    def term_near(c):
        return z_copy(proj.at[2], near_in, nsend.at[c], nrecv.at[c], partner, c)

    def term_up(c, k):
        return z_copy(proj.at[k], relay_in.at[k], rsend.at[c, k], rrecv.at[c, k], partner, c)

    def term_far(c, k):
        return z_copy(relay_out.at[k], far_in, fsend.at[c, k], frecv.at[c], far[k], c)

    def block_near(c):
        return z_copy(stream.at[mz], stream.at[mz], gsend.at[c], grecv.at[c], partner, c)

    def block_far(c):
        return z_copy(stream.at[mz], stream.at[mz], hsend.at[c], hrecv.at[c, rank], far_inner, c)

    def block_down(c, k):
        return z_copy(stream.at[far[k]], stream.at[far[k]], tsend.at[c, k], trecv.at[c, k], partner, c)

    def rows_of(c):
        return slice(c * piece, (c + 1) * piece)

    for c in range(chunks):

        @pl.when(outer)
        def _():
            for k in range(2):
                term_up(c, k).start()

        term_near(c).start()
    total[...] += project(mz)

    for c in range(chunks):
        at = rows_of(c)

        @pl.when(inner)
        def _():
            for k in range(2):
                term_up(c, k).wait_recv()
                relay_out[k, at, :] = (
                    proj[k, at, :].astype(F32) + relay_in[k, at, :].astype(F32)
                ).astype(BF16)
                term_far(c, k).start()

    for c in range(chunks):
        at = rows_of(c)
        term_near(c).wait_recv()
        term_far(c, 0).wait_recv()
        mine = (total[at, :] + near_in[at, :].astype(F32) + far_in[at, :].astype(F32)).astype(BF16)
        hid_out[at, :] = mine
        stream[mz, at, :] = mine
        block_far(c).start()
        block_near(c).start()

    def norm_chunk(c):
        at = rows_of(c)
        first = jnp.zeros((piece, 1), F32)
        second = jnp.zeros((piece, 1), F32)
        for j in range(shares):
            x = stream[j, at, :].astype(F32)
            first += jnp.sum(x, axis=1, keepdims=True)
            second += jnp.sum(x * x, axis=1, keepdims=True)
        mean = first / model
        scale = lax.rsqrt(second / model - mean * mean + 1e-05)
        for j in range(shares):
            columns = slice(j * share, (j + 1) * share)
            x = stream[j, at, :].astype(F32)
            normed[at, columns] = (
                (x - mean) * scale * gain_ref[:, columns] + nbias_ref[:, columns]
            ).astype(BF16)
        block = 256
        for j in range(qkv_out.shape[1] // block):
            columns = slice(j * block, (j + 1) * block)
            out = jnp.dot(normed[at, :], qw[:, columns], preferred_element_type=F32)
            qkv_out[at, columns] = (out + qbias_ref[columns][None, :]).astype(BF16)

    load_qw.wait()
    for c in range(chunks):

        @pl.when(inner)
        def _():
            for k in (1, 0):
                z_copy(
                    stream.at[far[k]], stream.at[far[k]], hsend.at[c], hrecv.at[c, k], far_inner, c
                ).wait_recv()
                block_down(c, k).start()

    for c in range(chunks):
        block_near(c).wait_recv()

        @pl.when(outer)
        def _():
            for k in range(2):
                block_down(c, k).wait_recv()

        norm_chunk(c)

    for c in range(chunks):
        term_near(c).wait_send()
        block_near(c).wait_send()
        block_far(c).wait_send()
        for k in range(2):
            pl.when(outer)(lambda: term_up(c, k).wait_send())
            pl.when(inner)(lambda: term_far(c, k).wait_send())
            pl.when(inner)(lambda: block_down(c, k).wait_send())


def hand_over(a_in, b_in, a_out, b_out):
    a_out[...] = a_in[...]
    b_out[...] = b_in[...]


def lookup(table_values, index_rows, count_all):
    matched = index_rows[..., None] == jnp.arange(count_all, dtype=jnp.int32)
    return jnp.sum(jnp.where(matched, table_values, 0), axis=-1)


def on_device(
    hidden, group_qkv, mlp_branch, key_cache, paged_value_cache, cache_lengths, page_table,
    dense_weight, dense_bias, norm_gain, norm_bias, qkv_weight, qkv_bias,
):
    tok_dev, share = hidden.shape
    pages = lax.axis_size("page")
    shares = lax.axis_size("head")
    me = lax.axis_index("page")
    requests = cache_lengths.shape[0]
    slots = key_cache.shape[0]
    heads = group_qkv.shape[1] // (3 * HEAD_SIZE)
    width = heads * HEAD_SIZE
    every = tok_dev * pages
    vmem = pl.BlockSpec(memory_space=pltpu.VMEM)
    anywhere = pl.BlockSpec(memory_space=pl.ANY)
    dma = pltpu.SemaphoreType.DMA

    global_rows = me * tok_dev + jnp.arange(tok_dev, dtype=jnp.int32)
    positions = lookup(cache_lengths, global_rows // GROUP, requests) + global_rows % GROUP
    lane = jnp.arange(HEAD_SIZE, dtype=jnp.int32)
    half = ROT // 2
    inverse = 1.0 / 10000.0 ** ((2 * (lane % half)).astype(F32) / ROT)
    angles = positions.astype(F32)[:, None] * inverse[None, :]
    turned = lane[None, :] < ROT
    sine = jnp.sin(angles)
    table = jnp.stack(
        [
            jnp.where(turned, jnp.cos(angles), 1.0),
            jnp.where(turned, jnp.where(lane[None, :] < half, -sine, sine), 0.0),
        ]
    )

    q_all, kv_all = pl.pallas_call(
        functools.partial(gather_kernel, heads),
        out_shape=(
            jax.ShapeDtypeStruct((every, width), BF16),
            jax.ShapeDtypeStruct((every, 2 * width), BF16),
        ),
        in_specs=[vmem, vmem],
        out_specs=(anywhere, anywhere),
        scratch_shapes=[
            pltpu.VMEM((tok_dev, width), BF16),
            pltpu.VMEM((tok_dev, 2 * width), BF16),
            dma((3, max(4, pages // 2))),
            dma((3, max(4, pages // 2))),
            dma((3, max(5, pages // 2))),
            dma((3, max(5, pages // 2))),
            dma((2,)),
        ],
        compiler_params=pltpu.CompilerParams(
            collective_id=0, has_side_effects=True, vmem_limit_bytes=LIMIT
        ),
        name="gather_qkv",
    )(group_qkv, table)

    factor = math.log2(math.e) / math.sqrt(HEAD_SIZE)
    smem = pl.BlockSpec(memory_space=pltpu.SMEM)
    key_out, value_out, partial, stats = pl.pallas_call(
        functools.partial(attention_kernel, heads, factor),
        out_shape=(
            jax.ShapeDtypeStruct(key_cache.shape, BF16),
            jax.ShapeDtypeStruct(key_cache.shape, BF16),
            jax.ShapeDtypeStruct((pages, width, tok_dev), BF16),
            jax.ShapeDtypeStruct((pages, 16, tok_dev), F32),
        ),
        in_specs=[smem, smem, anywhere, anywhere, anywhere, anywhere],
        out_specs=(anywhere, anywhere, vmem, vmem),
        scratch_shapes=[
            pltpu.VMEM((every, width), BF16),
            pltpu.VMEM((every, 2 * width), BF16),
            pltpu.VMEM(key_cache.shape, BF16),
            pltpu.VMEM(key_cache.shape, BF16),
            pltpu.VMEM((requests, width, GROUP), F32),
            pltpu.VMEM((requests, 8, GROUP), F32),
            pltpu.VMEM((requests, 8, GROUP), F32),
            pltpu.SMEM((slots + 1,), jnp.int32),
            dma((2, slots)),
            dma((2, slots)),
            dma((2,)),
        ],
        compiler_params=pltpu.CompilerParams(vmem_limit_bytes=LIMIT),
        name="attend_slots",
    )(cache_lengths, page_table, q_all, kv_all, key_cache, paged_value_cache)

    chips = pages // 2
    chunks = 2
    stream_share, projected = pl.pallas_call(
        functools.partial(tail_kernel, heads, chunks),
        out_shape=(
            jax.ShapeDtypeStruct(hidden.shape, BF16),
            jax.ShapeDtypeStruct(group_qkv.shape, BF16),
        ),
        in_specs=[vmem, vmem, vmem, vmem, anywhere, vmem, vmem, vmem, anywhere, vmem],
        out_specs=(vmem, vmem),
        scratch_shapes=[
            *[
                pltpu.VMEM((chips,) + shape, kind)
                for _ in range(3)
                for shape, kind in (((width, tok_dev), BF16), ((16, tok_dev), F32))
            ],
            pltpu.VMEM(dense_weight.shape, BF16),
            pltpu.VMEM(qkv_weight.shape, BF16),
            pltpu.VMEM((tok_dev, width), BF16),
            pltpu.VMEM((3, tok_dev, share), BF16),
            pltpu.VMEM((tok_dev, share), BF16),
            pltpu.VMEM((tok_dev, share), BF16),
            pltpu.VMEM((2, tok_dev, share), BF16),
            pltpu.VMEM((2, tok_dev, share), BF16),
            pltpu.VMEM((shares, tok_dev, share), BF16),
            pltpu.VMEM((tok_dev, share * shares), BF16),
            pltpu.VMEM((tok_dev, share), F32),
            dma((2,)),
            *[dma((2, chips)) for _ in range(4)],
            dma((chunks,)),
            dma((chunks,)),
            dma((chunks, 2)),
            dma((chunks,)),
            dma((chunks, 2)),
            dma((chunks, 2)),
            dma((chunks,)),
            dma((chunks,)),
            dma((chunks,)),
            dma((chunks, 2)),
            dma((chunks, 2)),
            dma((chunks, 2)),
        ],
        compiler_params=pltpu.CompilerParams(
            collective_id=1, has_side_effects=True, vmem_limit_bytes=LIMIT
        ),
        name="combine_project",
    )(
        partial, stats, hidden, mlp_branch, dense_weight, dense_bias[None, :], norm_gain[None, :],
        norm_bias[None, :], qkv_weight, qkv_bias,
    )
    new_hidden, next_qkv = pl.pallas_call(
        hand_over,
        out_shape=(
            jax.ShapeDtypeStruct(hidden.shape, BF16),
            jax.ShapeDtypeStruct(group_qkv.shape, BF16),
        ),
        in_specs=[vmem, vmem],
        out_specs=(vmem, vmem),
        name="hand_over",
    )(stream_share, projected)
    return new_hidden, next_qkv, key_out, value_out


def solution(mesh):
    in_specs = (
        P("page", "head"), P("page", "head"), P("page", "head"),
        P("page", None, "head"), P("page", None, "head"),
        P(), P(), P("head", None), P(), P(), P(), P(None, "head"), P("head"),
    )
    out_specs = (
        P("page", "head"), P("page", "head"), P("page", None, "head"), P("page", None, "head"),
    )
    return jax.shard_map(
        on_device, mesh=mesh, in_specs=in_specs, out_specs=out_specs, check_vma=False
    )
```

```python
import functools
import math

import jax
import jax.numpy as jnp
from jax import lax
from jax.experimental import pallas as pl
from jax.experimental.pallas import tpu as pltpu
from jax.sharding import PartitionSpec as P

HEAD_SIZE = 128
ROT = 32
PAGE_TOKENS = 128
GROUP = 512
MESH = pl.DeviceIdType.MESH
FLOOR = -1e29
MASKED = -1e30
LIMIT = 56 * 1024 * 1024
BF16 = jnp.bfloat16
F32 = jnp.float32


def signal_all(axes):
    barrier = pltpu.get_barrier_semaphore()
    count = 0
    for axis in axes:
        size = lax.axis_size(axis)
        me = lax.axis_index(axis)
        for offset in range(1, size):
            pl.semaphore_signal(
                barrier,
                inc=1,
                device_id={axis: lax.rem(me + offset, size)},
                device_id_type=MESH,
            )
            count += 1
    return barrier, count


def gather_kernel(heads, x_ref, table_ref, q_ref, kv_ref, q_mine, kv_mine, send, recv, fsend, frecv, lsem):
    pages = lax.axis_size("page")
    chips = pages // 2
    me = lax.axis_index("page")
    chip = lax.div(me, 2)
    core = lax.rem(me, 2)
    sibling = chip * 2 + 1 - core
    rows = x_ref.shape[0]
    width = heads * HEAD_SIZE
    lane = lax.broadcasted_iota(jnp.int32, (rows, HEAD_SIZE), 1)
    barrier, count = signal_all(("page",))

    def rotated(column):
        x = x_ref[:, column : column + HEAD_SIZE].astype(F32)
        ahead = pltpu.roll(x, HEAD_SIZE - ROT // 2, 1)
        behind = pltpu.roll(x, ROT // 2, 1)
        other = jnp.where(lane < ROT // 2, ahead, behind)
        return (x * table_ref[0] + other * table_ref[1]).astype(BF16)

    for head in range(heads):
        base = head * 3 * HEAD_SIZE
        at = head * HEAD_SIZE
        q_mine[:, at : at + HEAD_SIZE] = rotated(base)
        kv_mine[:, at : at + HEAD_SIZE] = rotated(base + HEAD_SIZE)
        kv_mine[:, width + at : width + at + HEAD_SIZE] = x_ref[
            :, base + 2 * HEAD_SIZE : base + 3 * HEAD_SIZE
        ]

    pieces = (
        (q_mine, q_ref, slice(0, width)),
        (kv_mine, kv_ref, slice(0, width)),
        (kv_mine, kv_ref, slice(width, 2 * width)),
    )

    def source_of(piece):
        src, _, columns = pieces[piece]
        return src.at[:, columns]

    def block_of(piece, index, begin=0, size=rows):
        _, dst, columns = pieces[piece]
        return dst.at[pl.ds(pl.multiple_of(index * rows + begin, 16), size), columns]

    def push(src, dst, target, send_sem, recv_sem):
        copy = pltpu.make_async_remote_copy(
            src_ref=src,
            dst_ref=dst,
            send_sem=send_sem,
            recv_sem=recv_sem,
            device_id={"page": target},
            device_id_type=MESH,
        )
        copy.start()
        return copy

    local = []
    for which, (src, dst) in enumerate(((q_mine, q_ref), (kv_mine, kv_ref))):
        copy = pltpu.make_async_copy(
            src, dst.at[pl.ds(pl.multiple_of(me * rows, rows), rows), :], lsem.at[which]
        )
        copy.start()
        local.append(copy)
    pl.semaphore_wait(barrier, count)

    first, forwards = [], []

    def forward(piece, index, kind, begin=0, size=rows):
        landed = block_of(piece, index, begin, size)
        forwards.append(push(landed, landed, sibling, fsend.at[piece, kind], frecv.at[piece, kind]))

    span = range(len(pieces))
    if chips == 4:
        x = lax.rem(chip, 2)
        across = (chip + 1 - 2 * x) * 2 + core
        along = lax.rem(chip + 2, 4) * 2 + core
        corner = lax.rem(chip + 3 - 2 * x, 4) * 2 + core
        half = rows // 2
        from_across, from_along = [], []
        for piece in span:
            src, dst = source_of(piece), block_of(piece, me)
            from_across.append(push(src, dst, across, send.at[piece, 0], recv.at[piece, 0]))
            from_along.append(push(src, dst, along, send.at[piece, 1], recv.at[piece, 1]))
            forwards.append(push(src, dst, sibling, fsend.at[piece, 0], frecv.at[piece, 0]))
        low, high = [], []
        for piece in span:
            from_across[piece].wait_recv()
            landed = block_of(piece, across, 0, half)
            low.append(push(landed, landed, along, send.at[piece, 2], recv.at[piece, 2]))
            from_along[piece].wait_recv()
            landed = block_of(piece, along, half, half)
            high.append(push(landed, landed, across, send.at[piece, 3], recv.at[piece, 3]))
            forward(piece, across, 1)
            forward(piece, along, 2)
        for piece in span:
            low[piece].wait_recv()
            forward(piece, corner, 3, 0, half)
            high[piece].wait_recv()
            forward(piece, corner, 4, half, half)
        first = from_across + from_along + low + high
    else:
        for piece in span:
            src, dst = source_of(piece), block_of(piece, me)
            for offset in range(1, chips):
                target = lax.rem(chip + offset, chips) * 2 + core
                first.append(push(src, dst, target, send.at[piece, offset], recv.at[piece, offset]))
            forwards.append(push(src, dst, sibling, fsend.at[piece, 0], frecv.at[piece, 0]))
        for piece in span:
            for offset in range(1, chips):
                first[piece * (chips - 1) + offset - 1].wait_recv()
                forward(piece, lax.rem(chip + chips - offset, chips) * 2 + core, offset)
    for copy in local:
        copy.wait()
    for copy in first:
        copy.wait_send()
    for copy in forwards:
        copy.wait()


def attention_kernel(
    heads, factor,
    len_ref, table_ref, q_hbm, kv_hbm, kc_hbm, vc_hbm,
    ko_hbm, vo_hbm, o_ref, st_ref,
    q_ref, kv_ref, keys, values, acc, m_s, l_s, code, in_sem, out_sem, q_sem,
):
    requests, max_pages = table_ref.shape
    slots = keys.shape[0]
    width = heads * HEAD_SIZE
    tok_dev = o_ref.shape[2]
    base = lax.axis_index("page") * slots

    load_q = pltpu.make_async_copy(q_hbm, q_ref, q_sem.at[0])
    load_kv = pltpu.make_async_copy(kv_hbm, kv_ref, q_sem.at[1])
    load_q.start()

    def page_in(slot):
        return (
            pltpu.make_async_copy(kc_hbm.at[slot], keys.at[slot], in_sem.at[0, slot]),
            pltpu.make_async_copy(vc_hbm.at[slot], values.at[slot], in_sem.at[1, slot]),
        )

    def page_out(slot):
        return (
            pltpu.make_async_copy(keys.at[slot], ko_hbm.at[slot], out_sem.at[0, slot]),
            pltpu.make_async_copy(values.at[slot], vo_hbm.at[slot], out_sem.at[1, slot]),
        )

    for slot in range(slots):
        for copy in page_in(slot):
            copy.start()
    load_kv.start()
    for slot in range(slots + 1):
        code[slot] = 0
    for r in range(requests):

        def place(i, _):
            slot = table_ref[r, i] - base
            held = (slot >= 0) & (slot < slots)
            code[jnp.where(held, slot, slots)] = r * max_pages + i + 1
            return 0

        lax.fori_loop(0, max_pages, place, 0)
    acc[...] = jnp.zeros_like(acc)
    m_s[...] = jnp.full_like(m_s, FLOOR)
    l_s[...] = jnp.zeros_like(l_s)
    load_q.wait()

    spans = [slice(head * HEAD_SIZE, (head + 1) * HEAD_SIZE) for head in range(heads)]

    def attend(slot, request, start, masked):
        mine = pl.ds(pl.multiple_of(request * GROUP, GROUP), GROUP)
        m_old = m_s[request, 0:heads, :]
        l_old = l_s[request, 0:heads, :]
        m_all, l_all, fades, parts = [], [], [], []
        for head, at in enumerate(spans):
            scores = (
                lax.dot_general(
                    keys[slot, :, at], q_ref[mine, at], (((1,), (1,)), ((), ())),
                    preferred_element_type=F32,
                )
                * factor
            )
            if masked:
                row = start + lax.broadcasted_iota(jnp.int32, scores.shape, 0)
                column = lax.broadcasted_iota(jnp.int32, scores.shape, 1)
                scores = jnp.where(row <= column, scores, MASKED)
            before = m_old[head : head + 1, :]
            m_new = jnp.maximum(before, jnp.max(scores, axis=0, keepdims=True))
            fade = jnp.exp2(before - m_new)
            weights = jnp.exp2(scores - m_new)
            m_all.append(m_new)
            l_all.append(l_old[head : head + 1, :] * fade + jnp.sum(weights, axis=0, keepdims=True))
            fades.append(fade)
            parts.append(
                lax.dot_general(
                    values[slot, :, at], weights.astype(BF16), (((0,), (0,)), ((), ())),
                    preferred_element_type=F32,
                )
            )
        for head, at in enumerate(spans):
            acc[request, at, :] = acc[request, at, :] * fades[head] + parts[head]
        m_s[request, 0:heads, :] = jnp.concatenate(m_all, axis=0)
        l_s[request, 0:heads, :] = jnp.concatenate(l_all, axis=0)

    def facts(slot):
        known = code[slot]
        entry = jnp.maximum(known - 1, 0)
        request = lax.div(entry, max_pages)
        start = lax.rem(entry, max_pages) * PAGE_TOKENS - len_ref[request]
        live = (known > 0) & (start < GROUP)
        return request, start, live & (start <= -PAGE_TOKENS), live & (start > -PAGE_TOKENS)

    def step(slot, _):
        for copy in page_in(slot):
            copy.wait()
        request, start, old, new = facts(slot)

        @pl.when(jnp.logical_not(new))
        def _():
            for copy in page_out(slot):
                copy.start()

        pl.when(old)(lambda: attend(slot, request, start, False))
        return 0

    lax.fori_loop(0, slots, step, 0)
    load_kv.wait()

    def fresh_step(slot, _):
        request, start, _, new = facts(slot)

        @pl.when(new)
        def _():
            mine = pl.ds(pl.multiple_of(request * GROUP, GROUP), GROUP)
            row = start + lax.broadcasted_iota(jnp.int32, (PAGE_TOKENS, GROUP), 0)
            column = lax.broadcasted_iota(jnp.int32, (PAGE_TOKENS, GROUP), 1)
            pick = jnp.where(row == column, 1.0, 0.0).astype(BF16)
            place = start + lax.broadcasted_iota(jnp.int32, (PAGE_TOKENS, width), 0)
            fresh = (place >= 0) & (place < GROUP)
            for part, held in enumerate((keys, values)):
                moved = jnp.dot(
                    pick, kv_ref[mine, part * width : (part + 1) * width], preferred_element_type=F32
                )
                held[slot] = jnp.where(fresh, moved, held[slot].astype(F32)).astype(BF16)
            for copy in page_out(slot):
                copy.start()
            attend(slot, request, start, True)

        return 0

    lax.fori_loop(0, slots, fresh_step, 0)

    per = GROUP // tok_dev
    for r in range(requests):
        for b in range(per):
            columns = slice(b * tok_dev, (b + 1) * tok_dev)
            o_ref[r * per + b] = acc[r, :, columns].astype(BF16)
            st_ref[r * per + b, 0:8, :] = m_s[r, :, columns]
            st_ref[r * per + b, 8:16, :] = l_s[r, :, columns]

    def drain(slot, _):
        for copy in page_out(slot):
            copy.wait()
        return 0

    lax.fori_loop(0, slots, drain, 0)


def tail_kernel(
    heads, chunks,
    o_ref, st_ref, hidden_ref, branch_ref, dw_ref, dbias_ref, gain_ref, nbias_ref, qw_ref, qbias_ref,
    hid_out, qkv_out,
    o_sib, st_sib, o_pair, st_pair, o_in, st_in, dw, qw, att, proj,
    near_in, far_in, relay_in, relay_out, stream, normed, total,
    wsem, bsend, brecv, osend, orecv,
    nsend, nrecv, fsend, frecv, rsend, rrecv, gsend, grecv, hsend, hrecv, tsend, trecv,
):
    pages = lax.axis_size("page")
    chips = pages // 2
    shares = lax.axis_size("head")
    me = lax.axis_index("page")
    mz = lax.axis_index("head")
    chip = lax.div(me, 2)
    core = lax.rem(me, 2)
    rows, share = hidden_ref.shape
    model = share * shares
    piece = rows // chunks

    load_dw = pltpu.make_async_copy(dw_ref, dw, wsem.at[0])
    load_qw = pltpu.make_async_copy(qw_ref, qw, wsem.at[1])
    load_dw.start()
    barrier, count = signal_all(("page", "head"))
    pl.semaphore_wait(barrier, count)

    def page_push(src, dst, target, send_sem, recv_sem):
        copy = pltpu.make_async_remote_copy(
            src_ref=src,
            dst_ref=dst,
            send_sem=send_sem,
            recv_sem=recv_sem,
            device_id={"page": target},
            device_id_type=MESH,
        )
        copy.start()
        return copy

    order = list(range(chips - 1, 0, -1)) + [0]
    shared = {}
    for k in order:
        theirs = lax.rem(chip + k, chips) * 2 + 1 - core
        shared[k] = (
            page_push(st_ref.at[theirs], st_sib.at[k], chip * 2 + 1 - core, bsend.at[0, k], brecv.at[0, k]),
            page_push(o_ref.at[theirs], o_sib.at[k], chip * 2 + 1 - core, bsend.at[1, k], brecv.at[1, k]),
        )
    load_qw.start()
    sent = []
    for k in order:
        for copy in shared[k]:
            copy.wait()
        ours = lax.rem(chip + k, chips) * 2 + core
        for head in range(heads):
            at = slice(head * HEAD_SIZE, (head + 1) * HEAD_SIZE)
            m_mine = st_ref[ours, head : head + 1, :]
            m_sib = st_sib[k, head : head + 1, :]
            peak = jnp.maximum(m_mine, m_sib)
            e_mine = jnp.exp2(m_mine - peak)
            e_sib = jnp.exp2(m_sib - peak)
            st_pair[k, head : head + 1, :] = peak
            st_pair[k, 8 + head : 9 + head, :] = (
                st_ref[ours, 8 + head : 9 + head, :] * e_mine + st_sib[k, 8 + head : 9 + head, :] * e_sib
            )
            o_pair[k, at, :] = (
                o_ref[ours, at, :].astype(F32) * e_mine + o_sib[k, at, :].astype(F32) * e_sib
            ).astype(BF16)
        if k:
            sent.append(page_push(st_pair.at[k], st_in.at[k], ours, osend.at[0, k], orecv.at[0, k]))
            sent.append(page_push(o_pair.at[k], o_in.at[k], ours, osend.at[1, k], orecv.at[1, k]))
    st_in[0] = st_pair[0]
    o_in[0] = o_pair[0]
    total[...] = dbias_ref[:, pl.ds(pl.multiple_of(mz * share, share), share)] + (
        hidden_ref[...].astype(F32) + branch_ref[...].astype(F32)
    )
    for copy in sent:
        copy.wait()

    for head in range(heads):
        at = slice(head * HEAD_SIZE, (head + 1) * HEAD_SIZE)

        def raise_peak(j, peak):
            return jnp.maximum(peak, st_in[j, head : head + 1, :])

        peak = lax.fori_loop(1, chips, raise_peak, st_in[0, head : head + 1, :])

        def add(j, pair):
            summed, count = pair
            scale = jnp.exp2(st_in[j, head : head + 1, :] - peak)
            return (
                summed + o_in[j, at, :].astype(F32) * scale,
                count + st_in[j, 8 + head : 9 + head, :] * scale,
            )

        summed, count = lax.fori_loop(
            0, chips, add, (jnp.zeros((HEAD_SIZE, rows), F32), jnp.zeros((1, rows), F32))
        )
        att[:, at] = (summed / count).T.astype(BF16)
    load_dw.wait()
    outer = (mz == 0) | (mz == shares - 1)
    inner = jnp.logical_not(outer)
    partner = mz + 1 - 2 * lax.rem(mz, 2)
    far_inner = jnp.where(mz < 2, 2, 1)
    far_outer = jnp.where(mz < 2, 3, 0)
    far = (far_outer, far_inner)
    rank = jnp.where(outer, 0, 1)

    def project(t):
        columns = pl.ds(pl.multiple_of(t * share, share), share)
        return jnp.dot(att[...], dw[:, columns], preferred_element_type=F32)

    for k, t in enumerate((*far, partner)):
        proj[k] = project(t).astype(BF16)

    def z_copy(src, dst, send_sem, recv_sem, target, c):
        at = pl.ds(c * piece, piece)
        return pltpu.make_async_remote_copy(
            src_ref=src.at[at, :],
            dst_ref=dst.at[at, :],
            send_sem=send_sem,
            recv_sem=recv_sem,
            device_id={"head": target},
            device_id_type=MESH,
        )

    def term_near(c):
        return z_copy(proj.at[2], near_in, nsend.at[c], nrecv.at[c], partner, c)

    def term_up(c, k):
        return z_copy(proj.at[k], relay_in.at[k], rsend.at[c, k], rrecv.at[c, k], partner, c)

    def term_far(c, k):
        return z_copy(relay_out.at[k], far_in, fsend.at[c, k], frecv.at[c], far[k], c)

    def block_near(c):
        return z_copy(stream.at[mz], stream.at[mz], gsend.at[c], grecv.at[c], partner, c)

    def block_far(c):
        return z_copy(stream.at[mz], stream.at[mz], hsend.at[c], hrecv.at[c, rank], far_inner, c)

    def block_down(c, k):
        return z_copy(stream.at[far[k]], stream.at[far[k]], tsend.at[c, k], trecv.at[c, k], partner, c)

    def rows_of(c):
        return slice(c * piece, (c + 1) * piece)

    for c in range(chunks):

        @pl.when(outer)
        def _():
            for k in range(2):
                term_up(c, k).start()

        term_near(c).start()
    total[...] += project(mz)

    def relay_sum(c):
        at = rows_of(c)

        @pl.when(inner)
        def _():
            for k in range(2):
                term_up(c, k).wait_recv()
                relay_out[k, at, :] = (
                    proj[k, at, :].astype(F32) + relay_in[k, at, :].astype(F32)
                ).astype(BF16)
                term_far(c, k).start()

    def finish(c):
        at = rows_of(c)
        term_near(c).wait_recv()
        term_far(c, 0).wait_recv()
        mine = (total[at, :] + near_in[at, :].astype(F32) + far_in[at, :].astype(F32)).astype(BF16)
        hid_out[at, :] = mine
        stream[mz, at, :] = mine
        block_far(c).start()
        block_near(c).start()

    def relay_block(c):
        @pl.when(inner)
        def _():
            for k in (1, 0):
                z_copy(
                    stream.at[far[k]], stream.at[far[k]], hsend.at[c], hrecv.at[c, k], far_inner, c
                ).wait_recv()
                block_down(c, k).start()

    def norm_chunk(c):
        at = rows_of(c)
        block_near(c).wait_recv()

        @pl.when(outer)
        def _():
            for k in range(2):
                block_down(c, k).wait_recv()

        first = jnp.zeros((piece, 1), F32)
        second = jnp.zeros((piece, 1), F32)
        for j in range(shares):
            x = stream[j, at, :].astype(F32)
            first += jnp.sum(x, axis=1, keepdims=True)
            second += jnp.sum(x * x, axis=1, keepdims=True)
        mean = first / model
        scale = lax.rsqrt(second / model - mean * mean + 1e-05)
        for j in range(shares):
            columns = slice(j * share, (j + 1) * share)
            x = stream[j, at, :].astype(F32)
            normed[at, columns] = (
                (x - mean) * scale * gain_ref[:, columns] + nbias_ref[:, columns]
            ).astype(BF16)

    def product(c):
        at = slice((c - 1) * piece, (c + 1) * piece)
        block = 256
        for j in range(qkv_out.shape[1] // block):
            columns = slice(j * block, (j + 1) * block)
            out = jnp.dot(normed[at, :], qw[:, columns], preferred_element_type=F32)
            qkv_out[at, columns] = (out + qbias_ref[columns][None, :]).astype(BF16)

    relay_sum(0)
    for c in range(chunks + 2):
        if c + 1 < chunks:
            relay_sum(c + 1)
        if c < chunks:
            finish(c)
        if 1 <= c <= chunks:
            relay_block(c - 1)
        if c >= 2:
            norm_chunk(c - 2)
            if c - 2 == 1:
                load_qw.wait()
            if (c - 2) % 2 == 1:
                product(c - 2)

    for c in range(chunks):
        term_near(c).wait_send()
        block_near(c).wait_send()
        block_far(c).wait_send()
        for k in range(2):
            pl.when(outer)(lambda: term_up(c, k).wait_send())
            pl.when(inner)(lambda: term_far(c, k).wait_send())
            pl.when(inner)(lambda: block_down(c, k).wait_send())


def hand_over(a_in, b_in, a_out, b_out):
    a_out[...] = a_in[...]
    b_out[...] = b_in[...]


def lookup(table_values, index_rows, count_all):
    matched = index_rows[..., None] == jnp.arange(count_all, dtype=jnp.int32)
    return jnp.sum(jnp.where(matched, table_values, 0), axis=-1)


def on_device(
    hidden, group_qkv, mlp_branch, key_cache, paged_value_cache, cache_lengths, page_table,
    dense_weight, dense_bias, norm_gain, norm_bias, qkv_weight, qkv_bias,
):
    tok_dev, share = hidden.shape
    pages = lax.axis_size("page")
    shares = lax.axis_size("head")
    me = lax.axis_index("page")
    requests = cache_lengths.shape[0]
    slots = key_cache.shape[0]
    heads = group_qkv.shape[1] // (3 * HEAD_SIZE)
    width = heads * HEAD_SIZE
    every = tok_dev * pages
    vmem = pl.BlockSpec(memory_space=pltpu.VMEM)
    anywhere = pl.BlockSpec(memory_space=pl.ANY)
    dma = pltpu.SemaphoreType.DMA

    global_rows = me * tok_dev + jnp.arange(tok_dev, dtype=jnp.int32)
    positions = lookup(cache_lengths, global_rows // GROUP, requests) + global_rows % GROUP
    lane = jnp.arange(HEAD_SIZE, dtype=jnp.int32)
    half = ROT // 2
    inverse = 1.0 / 10000.0 ** ((2 * (lane % half)).astype(F32) / ROT)
    angles = positions.astype(F32)[:, None] * inverse[None, :]
    turned = lane[None, :] < ROT
    sine = jnp.sin(angles)
    table = jnp.stack(
        [
            jnp.where(turned, jnp.cos(angles), 1.0),
            jnp.where(turned, jnp.where(lane[None, :] < half, -sine, sine), 0.0),
        ]
    )

    q_all, kv_all = pl.pallas_call(
        functools.partial(gather_kernel, heads),
        out_shape=(
            jax.ShapeDtypeStruct((every, width), BF16),
            jax.ShapeDtypeStruct((every, 2 * width), BF16),
        ),
        in_specs=[vmem, vmem],
        out_specs=(anywhere, anywhere),
        scratch_shapes=[
            pltpu.VMEM((tok_dev, width), BF16),
            pltpu.VMEM((tok_dev, 2 * width), BF16),
            dma((3, max(4, pages // 2))),
            dma((3, max(4, pages // 2))),
            dma((3, max(5, pages // 2))),
            dma((3, max(5, pages // 2))),
            dma((2,)),
        ],
        compiler_params=pltpu.CompilerParams(
            collective_id=0, has_side_effects=True, vmem_limit_bytes=LIMIT
        ),
        name="gather_qkv",
    )(group_qkv, table)

    factor = math.log2(math.e) / math.sqrt(HEAD_SIZE)
    smem = pl.BlockSpec(memory_space=pltpu.SMEM)
    key_out, value_out, partial, stats = pl.pallas_call(
        functools.partial(attention_kernel, heads, factor),
        out_shape=(
            jax.ShapeDtypeStruct(key_cache.shape, BF16),
            jax.ShapeDtypeStruct(key_cache.shape, BF16),
            jax.ShapeDtypeStruct((pages, width, tok_dev), BF16),
            jax.ShapeDtypeStruct((pages, 16, tok_dev), F32),
        ),
        in_specs=[smem, smem, anywhere, anywhere, anywhere, anywhere],
        out_specs=(anywhere, anywhere, vmem, vmem),
        scratch_shapes=[
            pltpu.VMEM((every, width), BF16),
            pltpu.VMEM((every, 2 * width), BF16),
            pltpu.VMEM(key_cache.shape, BF16),
            pltpu.VMEM(key_cache.shape, BF16),
            pltpu.VMEM((requests, width, GROUP), F32),
            pltpu.VMEM((requests, 8, GROUP), F32),
            pltpu.VMEM((requests, 8, GROUP), F32),
            pltpu.SMEM((slots + 1,), jnp.int32),
            dma((2, slots)),
            dma((2, slots)),
            dma((2,)),
        ],
        compiler_params=pltpu.CompilerParams(vmem_limit_bytes=LIMIT),
        name="attend_slots",
    )(cache_lengths, page_table, q_all, kv_all, key_cache, paged_value_cache)

    chips = pages // 2
    chunks = 4
    stream_share, projected = pl.pallas_call(
        functools.partial(tail_kernel, heads, chunks),
        out_shape=(
            jax.ShapeDtypeStruct(hidden.shape, BF16),
            jax.ShapeDtypeStruct(group_qkv.shape, BF16),
        ),
        in_specs=[vmem, vmem, vmem, vmem, anywhere, vmem, vmem, vmem, anywhere, vmem],
        out_specs=(vmem, vmem),
        scratch_shapes=[
            *[
                pltpu.VMEM((chips,) + shape, kind)
                for _ in range(3)
                for shape, kind in (((width, tok_dev), BF16), ((16, tok_dev), F32))
            ],
            pltpu.VMEM(dense_weight.shape, BF16),
            pltpu.VMEM(qkv_weight.shape, BF16),
            pltpu.VMEM((tok_dev, width), BF16),
            pltpu.VMEM((3, tok_dev, share), BF16),
            pltpu.VMEM((tok_dev, share), BF16),
            pltpu.VMEM((tok_dev, share), BF16),
            pltpu.VMEM((2, tok_dev, share), BF16),
            pltpu.VMEM((2, tok_dev, share), BF16),
            pltpu.VMEM((shares, tok_dev, share), BF16),
            pltpu.VMEM((tok_dev, share * shares), BF16),
            pltpu.VMEM((tok_dev, share), F32),
            dma((2,)),
            *[dma((2, chips)) for _ in range(4)],
            dma((chunks,)),
            dma((chunks,)),
            dma((chunks, 2)),
            dma((chunks,)),
            dma((chunks, 2)),
            dma((chunks, 2)),
            dma((chunks,)),
            dma((chunks,)),
            dma((chunks,)),
            dma((chunks, 2)),
            dma((chunks, 2)),
            dma((chunks, 2)),
        ],
        compiler_params=pltpu.CompilerParams(
            collective_id=1, has_side_effects=True, vmem_limit_bytes=LIMIT
        ),
        name="combine_project",
    )(
        partial, stats, hidden, mlp_branch, dense_weight, dense_bias[None, :], norm_gain[None, :],
        norm_bias[None, :], qkv_weight, qkv_bias,
    )
    new_hidden, next_qkv = pl.pallas_call(
        hand_over,
        out_shape=(
            jax.ShapeDtypeStruct(hidden.shape, BF16),
            jax.ShapeDtypeStruct(group_qkv.shape, BF16),
        ),
        in_specs=[vmem, vmem],
        out_specs=(vmem, vmem),
        name="hand_over",
    )(stream_share, projected)
    return new_hidden, next_qkv, key_out, value_out


def solution(mesh):
    in_specs = (
        P("page", "head"), P("page", "head"), P("page", "head"),
        P("page", None, "head"), P("page", None, "head"),
        P(), P(), P("head", None), P(), P(), P(), P(None, "head"), P("head"),
    )
    out_specs = (
        P("page", "head"), P("page", "head"), P("page", None, "head"), P("page", None, "head"),
    )
    return jax.shard_map(
        on_device, mesh=mesh, in_specs=in_specs, out_specs=out_specs, check_vma=False
    )
```
